32 devices in a mesh: grp: 2 (over x), req: 16 (over z, y, core).
Axes of the slice: x: 2, y: 2, z: 4, core: 2. Of those that a mesh axis runs over, the one named last changes fastest.
Arguments:
- xbc: bfloat16 [4096, 9216], P(('grp', 'req')), parts along dimension 0, may hold values from -6 to 6
- dt_raw: float32 [4096, 128], P(('grp', 'req')), parts along dimension 0, may hold values from -6 to 6
- conv_weight: float32 [4, 9216], replicated, may hold values from -3 to 3
- conv_bias: float32 [9216], replicated, may hold values from -3 to 3
- dt_bias: float32 [128], replicated, may hold values from -1 to 1
- a_log: float32 [128], replicated, may hold values from -6 to -2.5
- d_skip: float32 [128], replicated, may hold values from 0.5 to 1.5
- cache_states: bfloat16 [96, 128, 8192], P(('grp', 'req')), parts along dimension 0, may hold values from -24 to 24
- cache_tails: bfloat16 [96, 3, 9216], P(('grp', 'req')), parts along dimension 0, may hold values from -6 to 6
- hit_owner: int32 [32], P('grp'), parts along dimension 0, may hold values from 0 to 15, as said below
- hit_slot: int32 [32], P('grp'), parts along dimension 0, may hold values from 0 to 2, as said below
- hit_spans: int32 [32], P('grp'), parts along dimension 0, may hold values from 0 to 4
- request_of: int32 [32], P(('grp', 'req')), parts along dimension 0, may hold values from 0 to 15, each once
Outputs:
- y_out: bfloat16 [4096, 8192], P(('grp', 'req')), parts along dimension 0
- final_state: bfloat16 [32, 128, 8192], P(('grp', 'req')), parts along dimension 0
The draws below stay inside these ranges and needn't reach their ends.
There are 2 independent parts, one for each index of `grp`. The reference program is written for one: setup_inputs(seed, part) draws one part's arguments, and reference() takes and returns one part's arrays. A program takes and returns all parts, laid end to end along the dimension named above; an argument that names none is the same for every part. Nothing has to cross between parts.
Inputs may be any that keep to these rules, and one draw needn't show every extreme that they name: `hit_owner`: owners are skewed: some devices hold the prefixes of several requests, others of none. `hit_slot`: all requests that name the same owner device name the same slot of it. `request_of`: each request stands on exactly one device.
All inputs are finite; a program needn't handle non-finite values.
Results may differ from the reference program's by a relative error of at most 0.0039.
Values may be sent and summed in bfloat16 or wider, within the bound.
No kernel may reach another device: no remote copies, remote signals or barrier semaphores. Data moves between devices by JAX's collectives and lax.ppermute only.
A program may use at most 128 MiB of HBM per device.

```python
import jax
import jax.numpy as jnp
from jax import lax

HEADS = 128
HEAD_DIM = 64
GROUPS = 4
NST = 128
CONV_WIDTH = 4
SPAN = 128
SLOTS = 3
INNER = 8192
CONV_CH = 9216
REQUESTS = 16
ROWS = 2048
SLOTS_ALL = 48


def draw_hits(key):
    base = jax.random.fold_in(key, 17)
    first, second, third, fourth = jax.random.split(base, 4)
    left = jax.random.randint(first, (REQUESTS,), 0, REQUESTS)
    right = jax.random.randint(second, (REQUESTS,), 0, REQUESTS)
    skewed = left * right // REQUESTS
    order = jax.random.permutation(third, REQUESTS)
    owners = order[skewed]
    owners = owners.at[0].set(REQUESTS - 1)
    owners = owners.at[1].set(0)
    served = jax.random.randint(fourth, (REQUESTS,), 0, SLOTS)
    served = served.at[REQUESTS - 1].set(SLOTS - 1)
    served = served.at[0].set(0)
    slots = served[owners]
    return (owners.astype(jnp.int32), slots.astype(jnp.int32))


def draw_hit_owner(key, part):
    return draw_hits(key)[0]


def draw_hit_slot(key, part):
    return draw_hits(key)[1]


def plant(result, rng, smallest, largest):
    longest = result.shape.index(max(result.shape))
    spots = []
    for shift in (0, 1):
        where = [jax.random.randint(jax.random.fold_in(rng, axis), (), 0, length) for axis, length in enumerate(result.shape)]
        where[longest] = (where[longest] + shift) % result.shape[longest]
        spots.append(tuple(where))
    return result.at[spots[0]].set(smallest).at[spots[1]].set(largest)


def level_of(stream_key, shape, cuts, least, high):
    factor_of = 1.0
    for dim, shards_of in cuts:
        steps = jax.random.uniform(jax.random.fold_in(jax.random.fold_in(stream_key, 6), dim), (shards_of,), jnp.float32, least / len(cuts), high / len(cuts))
        factor_of = factor_of * jnp.repeat(jnp.exp(steps), shape[dim] // shards_of).reshape((-1,) + (1,) * (len(shape) - 1 - dim))
    return factor_of


def centred(stream_key, extent, scale, limit, cuts=(), dtype=jnp.bfloat16):
    loudness = level_of(stream_key, extent, cuts, -0.22, 0.18) if cuts else 1.0
    drawn = jax.random.normal(stream_key, extent, jnp.float32) * scale * loudness
    return jnp.minimum(jnp.maximum(drawn, -limit), limit).astype(dtype)


def setup_inputs(seed: int = 0, part: int = 0) -> dict:
    key_of = jax.random.split(jax.random.key(seed), 14)
    part_splits = jax.random.split(jax.random.fold_in(key_of[13], part), 14)
    xbc = centred(part_splits[0], (ROWS, CONV_CH), 1.0, 6.0, ((0, 16),))
    dt_raw = centred(part_splits[1], (ROWS, HEADS), 1.5, 6.0, ((0, 16),), jnp.float32)
    conv_weight = centred(key_of[2], (CONV_WIDTH, CONV_CH), CONV_WIDTH ** -0.5, 3.0, (), jnp.float32)
    conv_bias = centred(key_of[3], (CONV_CH,), 0.5, 3.0, (), jnp.float32)
    dt_bias = jnp.clip(jax.random.uniform(key_of[4], (HEADS,), jnp.float32, -1.0, 1.0), -1.0, 1.0)
    a_log = jnp.clip(jax.random.uniform(key_of[5], (HEADS,), jnp.float32, -6.0, -2.5), -6.0, -2.5)
    d_skip = jnp.clip(jax.random.uniform(key_of[6], (HEADS,), jnp.float32, 0.5, 1.5), 0.5, 1.5)
    cache_states = centred(part_splits[7], (SLOTS_ALL, NST, INNER), 4.0, 24.0, ((0, 16),))
    cache_tails = centred(part_splits[8], (SLOTS_ALL, CONV_WIDTH - 1, CONV_CH), 1.0, 6.0, ((0, 16),))
    hit_owner = draw_hit_owner(jax.random.fold_in(jax.random.fold_in(key_of[13], part), 71), part)
    hit_slot = draw_hit_slot(jax.random.fold_in(jax.random.fold_in(key_of[13], part), 71), part)
    hit_spans = plant(jax.random.randint(part_splits[11], (REQUESTS,), 0, 5), jax.random.fold_in(part_splits[11], 1), 0, 4).astype(jnp.int32)
    request_of = jax.random.permutation(part_splits[12], REQUESTS).astype(jnp.int32)
    return {"xbc": xbc, "dt_raw": dt_raw, "conv_weight": conv_weight, "conv_bias": conv_bias, "dt_bias": dt_bias, "a_log": a_log, "d_skip": d_skip, "cache_states": cache_states, "cache_tails": cache_tails, "hit_owner": hit_owner, "hit_slot": hit_slot, "hit_spans": hit_spans, "request_of": request_of}


def scan_request(xrows, dt_rows, tail, start, conv_weight, conv_bias, dt_bias, a_log, d_skip):
    rows = xrows.shape[0]
    taps = conv_weight.shape[0]
    per_group = HEADS // GROUPS
    extended = jnp.concatenate([tail, xrows], axis=0).astype(jnp.float32)
    conv = jnp.zeros((rows, xrows.shape[1]), jnp.float32) + conv_bias[None, :]
    for k in range(taps):
        conv = conv + conv_weight[k][None, :] * extended[k:k + rows]
    conv_out = jax.nn.silu(conv).astype(jnp.bfloat16)
    inputs = conv_out[:, :INNER].reshape(rows, GROUPS, per_group, HEAD_DIM).astype(jnp.float32)
    b_part = conv_out[:, INNER:INNER + GROUPS * NST].reshape(rows, GROUPS, NST).astype(jnp.float32)
    c_part = conv_out[:, INNER + GROUPS * NST:].reshape(rows, GROUPS, NST).astype(jnp.float32)
    step = jax.nn.softplus(dt_rows + dt_bias[None, :])
    cum = jnp.cumsum(step * (-jnp.exp(a_log))[None, :], axis=0)
    scores = jnp.einsum('tgn,sgn->gts', c_part, b_part)
    diff = cum.T[:, :, None] - cum.T[:, None, :]
    causal = lax.broadcasted_iota(jnp.int32, (rows, rows), 0) >= lax.broadcasted_iota(jnp.int32, (rows, rows), 1)
    decay = jnp.where(causal[None], jnp.exp(jnp.minimum(diff, 0.0)), 0.0)
    mixing = (scores[:, None] * decay.reshape(GROUPS, per_group, rows, rows)
              * step.T.reshape(GROUPS, per_group, 1, rows)).astype(jnp.bfloat16)
    y_intra = jnp.einsum('gjts,sgjp->tgjp', mixing.astype(jnp.float32), inputs)
    start_f = start.reshape(NST, GROUPS, per_group, HEAD_DIM).astype(jnp.float32)
    y_state = jnp.einsum('tgn,ngjp->tgjp', c_part, start_f) * jnp.exp(cum).reshape(rows, GROUPS, per_group, 1)
    skip = d_skip.reshape(1, GROUPS, per_group, 1) * inputs
    y_out = (y_intra + y_state + skip).reshape(rows, INNER).astype(jnp.bfloat16)
    last = cum[rows - 1]
    carried = ((jnp.exp(last[None, :] - cum) * step).reshape(rows, GROUPS, per_group, 1) * inputs).astype(jnp.bfloat16)
    fresh = jnp.einsum('sgn,sgjp->ngjp', b_part, carried.astype(jnp.float32))
    kept = jnp.exp(last).reshape(1, GROUPS, per_group, 1) * start_f
    final = (kept + fresh).reshape(NST, INNER).astype(jnp.bfloat16)
    return y_out, final


def reference(xbc, dt_raw, conv_weight, conv_bias, dt_bias, a_log, d_skip, cache_states, cache_tails, hit_owner, hit_slot, hit_spans, request_of):
    def one_request(item):
        xrows, dt_rows, request = item
        row = (hit_owner[request] * SLOTS + hit_slot[request]).astype(jnp.int32)
        live = hit_spans[request] > 0
        tail_row = lax.dynamic_index_in_dim(cache_tails, row, 0, keepdims=False)
        state_row = lax.dynamic_index_in_dim(cache_states, row, 0, keepdims=False)
        tail = jnp.where(live, tail_row, jnp.zeros_like(tail_row))
        start = jnp.where(live, state_row, jnp.zeros_like(state_row))
        return scan_request(xrows, dt_rows, tail, start, conv_weight, conv_bias, dt_bias, a_log, d_skip)

    outputs, finals = lax.map(one_request, (xbc.reshape(REQUESTS, SPAN, CONV_CH),
                                           dt_raw.reshape(REQUESTS, SPAN, HEADS), request_of))
    return outputs.reshape(ROWS, INNER), finals
```

```python
import functools

import jax
import jax.numpy as jnp
from jax import lax
from jax.experimental import pallas as pl
from jax.experimental.pallas import tpu as pltpu
from jax.sharding import PartitionSpec as P

HEADS = 128
HEAD_DIM = 64
GROUPS = 4
NST = 128
INNER = 8192
SPAN = 128
PER_GROUP = HEADS // GROUPS
CHUNK = 512
CHUNK_HEADS = CHUNK // HEAD_DIM
CHUNKS = INNER // CHUNK
GROUP_CHUNKS = CHUNKS // GROUPS


def pack_kernel(pieces, device_ref, owner_ref, slot_ref, request_ref, cache_ref, out_ref, request_out, sems):
    device = device_ref[0]
    served = jnp.int32(0)
    for r in range(owner_ref.shape[0]):
        served = jnp.where(owner_ref[r] == device, jnp.maximum(served, slot_ref[r]), served)
    width = INNER // pieces
    copies = [
        pltpu.make_async_copy(cache_ref.at[served, :, pl.ds(p * width, width)], out_ref.at[p], sems.at[p])
        for p in range(pieces)
    ]
    for copy in copies:
        copy.start()
    request_out[0] = request_ref[0]
    for copy in copies:
        copy.wait()


def pack(device, hit_owner, hit_slot, request_of, cache_states, pieces):
    smem = pl.BlockSpec(memory_space=pltpu.SMEM)
    hbm = pl.BlockSpec(memory_space=pl.ANY)
    return pl.pallas_call(
        functools.partial(pack_kernel, pieces),
        out_shape=(
            jax.ShapeDtypeStruct((pieces, NST, INNER // pieces), jnp.bfloat16),
            jax.ShapeDtypeStruct((1,), jnp.int32),
        ),
        in_specs=[smem, smem, smem, smem, hbm],
        out_specs=(hbm, smem),
        scratch_shapes=[pltpu.SemaphoreType.DMA((pieces,))],
        name="pack",
    )(device, hit_owner, hit_slot, request_of, cache_states)


def choose_kernel(pieces, wanted_ref, parts_ref, out_ref, sems):
    copies = [
        pltpu.make_async_copy(parts_ref.at[wanted_ref[p]], out_ref.at[p], sems.at[p]) for p in range(pieces)
    ]
    for copy in copies:
        copy.start()
    for copy in copies:
        copy.wait()


def choose(wanted, parts):
    pieces = parts.shape[0]
    smem = pl.BlockSpec(memory_space=pltpu.SMEM)
    hbm = pl.BlockSpec(memory_space=pl.ANY)
    return pl.pallas_call(
        functools.partial(choose_kernel, pieces),
        out_shape=jax.ShapeDtypeStruct(parts.shape, parts.dtype),
        in_specs=[smem, hbm],
        out_specs=hbm,
        scratch_shapes=[pltpu.SemaphoreType.DMA((pieces,))],
        name="choose",
    )(wanted, parts)


def convolved(x_ref, tail_ref, weight_ref, bias_ref):
    extended = jnp.concatenate([tail_ref[...], x_ref[...].astype(jnp.float32)], axis=0)
    total = bias_ref[...] + weight_ref[3:4, :] * extended[8:]
    for back in range(1, 4):
        total = total + weight_ref[3 - back : 4 - back, :] * pltpu.roll(extended, back, 0)[8:]
    return total / (1.0 + jnp.exp(-total))


def local_kernel(
    x_ref, xb_ref, xc_ref, tail_ref, tailb_ref, tailc_ref, w_ref, wb_ref, wc_ref, b_ref, bb_ref, bc_ref,
    dt_ref, dt_bias_ref, a_log_ref, skip_ref,
    y_ref, fresh_ref, c_out_ref, grown_ref,
    cum_cols, cum_rows, step_rows, carry_cols, scores, b_state,
):
    i = pl.program_id(0)
    rows = SPAN
    t_of = lax.broadcasted_iota(jnp.int32, (rows, rows), 0)
    s_of = lax.broadcasted_iota(jnp.int32, (rows, rows), 1)

    @pl.when(i == 0)
    def _():
        v = dt_ref[...] + dt_bias_ref[...]
        step = jnp.maximum(v, 0.0) + jnp.log1p(jnp.exp(-jnp.abs(v)))
        rate = -jnp.exp(a_log_ref[...])
        cum = step * rate
        shift = 1
        while shift < rows:
            cum = cum + jnp.where(t_of >= shift, pltpu.roll(cum, shift, 0), 0.0)
            shift *= 2
        grown_ref[...] = jnp.exp(cum)
        carry = jnp.exp(cum[rows - 1 : rows, :] - cum) * step
        for c in range(CHUNKS):
            cum_cols[c] = cum[:, c * CHUNK_HEADS : (c + 1) * CHUNK_HEADS]
            carry_cols[c] = carry[:, c * CHUNK_HEADS : (c + 1) * CHUNK_HEADS]
        cum_rows[...] = cum.T
        step_rows[...] = step.T

    @pl.when(i % GROUP_CHUNKS == 0)
    def _():
        b_part = convolved(xb_ref, tailb_ref, wb_ref, bb_ref).astype(jnp.bfloat16)
        c_part = convolved(xc_ref, tailc_ref, wc_ref, bc_ref).astype(jnp.bfloat16)
        b_state[...] = b_part
        c_out_ref[...] = c_part
        both = lax.dot_general(c_part, b_part, (((1,), (1,)), ((), ())), preferred_element_type=jnp.float32)
        scores[...] = jnp.where(t_of >= s_of, both, 0.0)

    x = convolved(x_ref, tail_ref, w_ref, b_ref).astype(jnp.bfloat16)
    x32 = x.astype(jnp.float32)
    first = pl.multiple_of(i * CHUNK_HEADS, CHUNK_HEADS)
    cum_r = cum_rows[pl.ds(first, CHUNK_HEADS), :]
    step_r = step_rows[pl.ds(first, CHUNK_HEADS), :]
    cum_c = cum_cols[i]
    carry_c = carry_cols[i]
    low = lax.broadcasted_iota(jnp.int32, (rows, 128), 1) < HEAD_DIM
    zero = jnp.zeros((rows, 128), jnp.bfloat16)
    for pair in range(CHUNK_HEADS // 2):
        mixes = []
        for j in (2 * pair, 2 * pair + 1):
            diff = cum_c[:, j : j + 1] - cum_r[j : j + 1, :]
            mixes.append((scores[...] * jnp.exp(jnp.minimum(diff, 0.0)) * step_r[j : j + 1, :]).astype(jnp.bfloat16))
        xp = x[:, pair * 128 : (pair + 1) * 128]
        stacked = jnp.concatenate([jnp.where(low, xp, zero), jnp.where(low, zero, xp)], axis=0)
        y = jnp.dot(jnp.concatenate(mixes, axis=1), stacked, preferred_element_type=jnp.float32)
        cols = slice(pair * 128, (pair + 1) * 128)
        y_ref[:, cols] = y + skip_ref[:, cols] * x32[:, cols]
        weight = jnp.where(low, carry_c[:, 2 * pair : 2 * pair + 1], carry_c[:, 2 * pair + 1 : 2 * pair + 2])
        carried = (weight * x32[:, cols]).astype(jnp.bfloat16)
        fresh_ref[:, cols] = lax.dot_general(
            b_state[...], carried, (((0,), (0,)), ((), ())), preferred_element_type=jnp.float32
        )


def local_part(xbc, tail, conv_weight, conv_bias, dt_raw, dt_bias, a_log, skip):
    rows = xbc.shape[0]
    bias = conv_bias[None, :]
    base = INNER // 128

    def blocks(height):
        return [
            pl.BlockSpec((height, CHUNK), lambda i: (0, i)),
            pl.BlockSpec((height, 128), lambda i: (0, base + i // GROUP_CHUNKS)),
            pl.BlockSpec((height, 128), lambda i: (0, base + GROUPS + i // GROUP_CHUNKS)),
        ]

    whole = lambda *shape: pl.BlockSpec(shape, lambda i: (0, 0))
    return pl.pallas_call(
        local_kernel,
        grid=(CHUNKS,),
        out_shape=(
            jax.ShapeDtypeStruct((rows, INNER), jnp.float32),
            jax.ShapeDtypeStruct((NST, INNER), jnp.float32),
            jax.ShapeDtypeStruct((rows, GROUPS * NST), jnp.bfloat16),
            jax.ShapeDtypeStruct((rows, HEADS), jnp.float32),
        ),
        in_specs=blocks(rows) + blocks(8) + blocks(4) + blocks(1)
        + [whole(rows, HEADS), whole(1, HEADS), whole(1, HEADS), pl.BlockSpec((1, CHUNK), lambda i: (0, i))],
        out_specs=(
            pl.BlockSpec((rows, CHUNK), lambda i: (0, i)),
            pl.BlockSpec((NST, CHUNK), lambda i: (0, i)),
            pl.BlockSpec((rows, NST), lambda i: (0, i // GROUP_CHUNKS)),
            whole(rows, HEADS),
        ),
        scratch_shapes=[
            pltpu.VMEM((CHUNKS, rows, CHUNK_HEADS), jnp.float32),
            pltpu.VMEM((HEADS, rows), jnp.float32),
            pltpu.VMEM((HEADS, rows), jnp.float32),
            pltpu.VMEM((CHUNKS, rows, CHUNK_HEADS), jnp.float32),
            pltpu.VMEM((rows, rows), jnp.float32),
            pltpu.VMEM((rows, NST), jnp.bfloat16),
        ],
        compiler_params=pltpu.CompilerParams(vmem_limit_bytes=24 * 1024 * 1024),
        cost_estimate=pl.CostEstimate(flops=2 * 300_000_000, bytes_accessed=14_000_000, transcendentals=4_000_000),
        name="local_part",
    )(
        xbc, xbc, xbc, tail, tail, tail, conv_weight, conv_weight, conv_weight, bias, bias, bias,
        dt_raw, dt_bias[None, :], a_log[None, :], skip,
    )


def state_kernel(width, live_ref, start_ref, c_ref, grown_ref, last_ref, y_ref, fresh_ref, y_out_ref, final_ref):
    live = live_ref[0] > 0
    start = jnp.where(live, start_ref[0], jnp.zeros(start_ref.shape[1:], start_ref.dtype))
    grown = grown_ref[0]
    y_state = jnp.dot(c_ref[...], start, preferred_element_type=jnp.float32)
    low = lax.broadcasted_iota(jnp.int32, (SPAN, 128), 1) < HEAD_DIM
    for pair in range(width // 128):
        cols = slice(pair * 128, (pair + 1) * 128)
        growth = jnp.where(low, grown[:, 2 * pair : 2 * pair + 1], grown[:, 2 * pair + 1 : 2 * pair + 2])
        y_out_ref[:, cols] = (y_ref[:, cols] + growth * y_state[:, cols]).astype(jnp.bfloat16)
    kept = last_ref[...] * start.astype(jnp.float32)
    final_ref[0] = (kept + fresh_ref[...]).astype(jnp.bfloat16)


def state_part(live, start, c_part, grown, y_local, fresh):
    pieces, _, width = start.shape
    rows = y_local.shape[0]
    heads = width // HEAD_DIM
    per_group = pieces // GROUPS
    grown_cols = grown.reshape(rows, pieces, heads).transpose(1, 0, 2)
    last = jnp.repeat(grown[rows - 1], HEAD_DIM)[None, :]
    return pl.pallas_call(
        functools.partial(state_kernel, width),
        grid=(pieces,),
        out_shape=(
            jax.ShapeDtypeStruct((rows, INNER), jnp.bfloat16),
            jax.ShapeDtypeStruct((1, NST, INNER), jnp.bfloat16),
        ),
        in_specs=[
            pl.BlockSpec(memory_space=pltpu.SMEM),
            pl.BlockSpec((1, NST, width), lambda i: (i, 0, 0)),
            pl.BlockSpec((rows, NST), lambda i: (0, i // per_group)),
            pl.BlockSpec((1, rows, heads), lambda i: (i, 0, 0)),
            pl.BlockSpec((1, width), lambda i: (0, i)),
            pl.BlockSpec((rows, width), lambda i: (0, i)),
            pl.BlockSpec((NST, width), lambda i: (0, i)),
        ],
        out_specs=(
            pl.BlockSpec((rows, width), lambda i: (0, i)),
            pl.BlockSpec((1, NST, width), lambda i: (0, 0, i)),
        ),
        cost_estimate=pl.CostEstimate(flops=2 * 134_000_000, bytes_accessed=14_000_000, transcendentals=0),
        name="state_part",
    )(live, start, c_part, grown_cols, last, y_local, fresh)


def local(
    xbc, dt_raw, conv_weight, conv_bias, dt_bias, a_log, d_skip, cache_states, cache_tails,
    hit_owner, hit_slot, hit_spans, request_of,
):
    pieces = hit_owner.shape[0]
    device = lax.axis_index("req")
    packed, request = pack(device[None].astype(jnp.int32), hit_owner, hit_slot, request_of, cache_states, pieces)
    parts = lax.all_to_all(packed, "req", split_axis=0, concat_axis=0, tiled=True)

    served = jnp.max(jnp.where(hit_owner == device, hit_slot, 0))
    every_tail = lax.all_gather(cache_tails[served], "req", axis=0, tiled=False)
    mine = request_of[0]
    live = (hit_spans[mine] > 0).astype(jnp.int32)
    tail = lax.dynamic_index_in_dim(every_tail, hit_owner[mine], 0, keepdims=False)
    tail = jnp.where(live > 0, tail, jnp.zeros_like(tail)).astype(jnp.float32)
    tail = jnp.pad(tail, ((8 - tail.shape[0], 0), (0, 0)))

    every_request = lax.all_gather(request, "req", axis=0, tiled=True)
    chosen = choose(hit_owner[every_request], parts)
    start = lax.all_to_all(chosen, "req", split_axis=0, concat_axis=0, tiled=True)

    skip = jnp.repeat(d_skip, HEAD_DIM)[None, :]
    y_local, fresh, c_part, grown = local_part(xbc, tail, conv_weight, conv_bias, dt_raw, dt_bias, a_log, skip)
    return state_part(live[None], start, c_part, grown, y_local, fresh)


def solution(mesh):
    in_specs = (
        P(("grp", "req"), None),
        P(("grp", "req"), None),
        P(),
        P(),
        P(),
        P(),
        P(),
        P(("grp", "req"), None, None),
        P(("grp", "req"), None, None),
        P("grp"),
        P("grp"),
        P("grp"),
        P(("grp", "req")),
    )
    out_specs = (P(("grp", "req"), None), P(("grp", "req"), None, None))
    return jax.shard_map(local, mesh=mesh, in_specs=in_specs, out_specs=out_specs, check_vma=False)
```

```python
import functools

import jax
import jax.numpy as jnp
from jax import lax
from jax.experimental import pallas as pl
from jax.experimental.pallas import tpu as pltpu
from jax.sharding import PartitionSpec as P

HEADS = 128
HEAD_DIM = 64
GROUPS = 4
NST = 128
INNER = 8192
SPAN = 128
PER_GROUP = HEADS // GROUPS
CHUNK = 512
CHUNK_HEADS = CHUNK // HEAD_DIM
CHUNKS = INNER // CHUNK
GROUP_CHUNKS = CHUNKS // GROUPS
LINES = 4
NOTE = 8
SMALL = pl.CostEstimate(flops=1000, bytes_accessed=1000, transcendentals=0)


def served_slot(device, owner_ref, slot_ref):
    served = jnp.int32(0)
    for r in range(owner_ref.shape[0]):
        served = jnp.where(owner_ref[r] == device, jnp.maximum(served, slot_ref[r]), served)
    return served


def tail_kernel(device_ref, owner_ref, slot_ref, tails_ref, out_ref, sem):
    served = served_slot(device_ref[0], owner_ref, slot_ref)
    copy = pltpu.make_async_copy(tails_ref.at[served], out_ref, sem)
    copy.start()
    copy.wait()


def served_tail(device, hit_owner, hit_slot, cache_tails):
    smem = pl.BlockSpec(memory_space=pltpu.SMEM)
    return pl.pallas_call(
        tail_kernel,
        out_shape=jax.ShapeDtypeStruct(cache_tails.shape[1:], cache_tails.dtype),
        in_specs=[smem, smem, smem, pl.BlockSpec(memory_space=pl.ANY)],
        out_specs=pl.BlockSpec(memory_space=pltpu.VMEM),
        scratch_shapes=[pltpu.SemaphoreType.DMA],
        cost_estimate=SMALL,
        name="served_tail",
    )(device, hit_owner, hit_slot, cache_tails)


def pack_kernel(device_ref, owner_ref, slot_ref, request_ref, cache_ref, out_ref, held, sems_in, sems_out):
    pieces, _, width = held.shape
    served = served_slot(device_ref[0], owner_ref, slot_ref)
    into, outof = [], []
    for p in range(pieces):
        source = cache_ref.at[served, :, pl.ds(p * width, width)]
        into.append(pltpu.make_async_copy(source, held.at[p, pl.ds(0, NST)], sems_in.at[p]))
        outof.append(pltpu.make_async_copy(held.at[p], out_ref.at[p], sems_out.at[p]))
    for copy in into:
        copy.start()
    note = jnp.full((NOTE, width), owner_ref[request_ref[0]].astype(jnp.float32)).astype(jnp.bfloat16)
    for p in range(pieces):
        held[p, NST:, :] = note
    for first, second in zip(into, outof):
        first.wait()
        second.start()
    for copy in outof:
        copy.wait()


def pack(device, hit_owner, hit_slot, request_of, cache_states, pieces):
    smem = pl.BlockSpec(memory_space=pltpu.SMEM)
    hbm = pl.BlockSpec(memory_space=pl.ANY)
    shape = (pieces, NST + NOTE, INNER // pieces)
    return pl.pallas_call(
        pack_kernel,
        out_shape=jax.ShapeDtypeStruct(shape, jnp.bfloat16),
        in_specs=[smem] * 4 + [hbm],
        out_specs=hbm,
        scratch_shapes=[
            pltpu.VMEM(shape, jnp.bfloat16),
            pltpu.SemaphoreType.DMA((pieces,)),
            pltpu.SemaphoreType.DMA((pieces,)),
        ],
        compiler_params=pltpu.CompilerParams(vmem_limit_bytes=56 * 1024 * 1024),
        cost_estimate=SMALL,
        name="pack",
    )(device, hit_owner, hit_slot, request_of, cache_states)


def choose_kernel(lines, device_ref, parts_ref, *refs):
    tails, refs = refs[:lines], refs[lines:]
    out_ref, wanted_ref, offered, (held, sems_in, sems_out) = refs[0], refs[1], refs[2 : 2 + LINES], refs[2 + LINES :]
    pieces = held.shape[0]
    into = [pltpu.make_async_copy(parts_ref.at[p], held.at[p], sems_in.at[p]) for p in range(pieces)]
    for copy in into:
        copy.start()
    for copy in into:
        copy.wait()
    outof = []
    for p in range(pieces):
        wanted = jnp.max(held[p, NST:, :128].astype(jnp.float32)).astype(jnp.int32)
        wanted_ref[p] = wanted
        copy = pltpu.make_async_copy(held.at[wanted, pl.ds(0, NST)], out_ref.at[p], sems_out.at[p])
        copy.start()
        outof.append(copy)
    device = device_ref[0]
    for k in range(LINES):
        apart = lax.bitwise_xor(wanted_ref[lax.bitwise_xor(device, k)], device)
        for m in range(lines):

            @pl.when(lax.div(apart, LINES) == m)
            def _(k=k, m=m):
                offered[k][...] = tails[m][...]

    for copy in outof:
        copy.wait()


def choose(device, parts, tails):
    pieces, _, width = parts.shape
    smem = pl.BlockSpec(memory_space=pltpu.SMEM)
    vmem = pl.BlockSpec(memory_space=pltpu.VMEM)
    hbm = pl.BlockSpec(memory_space=pl.ANY)
    tail = jax.ShapeDtypeStruct(tails[0].shape, tails[0].dtype)
    chosen, wanted, *offered = pl.pallas_call(
        functools.partial(choose_kernel, len(tails)),
        out_shape=[
            jax.ShapeDtypeStruct((pieces, NST, width), jnp.bfloat16),
            jax.ShapeDtypeStruct((pieces,), jnp.int32),
            *[tail] * LINES,
        ],
        in_specs=[smem, hbm] + [vmem] * len(tails),
        out_specs=[hbm, smem] + [vmem] * LINES,
        scratch_shapes=[
            pltpu.VMEM(parts.shape, jnp.bfloat16),
            pltpu.SemaphoreType.DMA((pieces,)),
            pltpu.SemaphoreType.DMA((pieces,)),
        ],
        compiler_params=pltpu.CompilerParams(vmem_limit_bytes=56 * 1024 * 1024),
        cost_estimate=SMALL,
        name="choose",
    )(device, parts, *tails)
    return chosen, wanted, offered


def convolved(x_ref, tail_ref, weight_ref, bias_ref):
    extended = jnp.concatenate([tail_ref[...], x_ref[...].astype(jnp.float32)], axis=0)
    total = bias_ref[...] + weight_ref[3:4, :] * extended[8:]
    for back in range(1, 4):
        total = total + weight_ref[3 - back : 4 - back, :] * pltpu.roll(extended, back, 0)[8:]
    return total / (1.0 + jnp.exp(-total))


def local_kernel(
    x_ref, xb_ref, xc_ref, tail_ref, tailb_ref, tailc_ref, w_ref, wb_ref, wc_ref, b_ref, bb_ref, bc_ref,
    dt_ref, dt_bias_ref, a_log_ref, skip_ref,
    y_ref, fresh_ref, c_out_ref, growth_ref,
    cum_cols, grown_cols, cum_rows, step_rows, carry_cols, scores, b_state,
    *, base,
):
    i = base + pl.program_id(0)
    rows = SPAN
    t_of = lax.broadcasted_iota(jnp.int32, (rows, rows), 0)
    s_of = lax.broadcasted_iota(jnp.int32, (rows, rows), 1)

    @pl.when(pl.program_id(0) == 0)
    def _():
        v = dt_ref[...] + dt_bias_ref[...]
        step = jnp.maximum(v, 0.0) + jnp.log1p(jnp.exp(-jnp.abs(v)))
        rate = -jnp.exp(a_log_ref[...])
        cum = step * rate
        shift = 1
        while shift < rows:
            cum = cum + jnp.where(t_of >= shift, pltpu.roll(cum, shift, 0), 0.0)
            shift *= 2
        grown = jnp.exp(cum)
        carry = jnp.exp(cum[rows - 1 : rows, :] - cum) * step
        for c in range(CHUNKS):
            cum_cols[c] = cum[:, c * CHUNK_HEADS : (c + 1) * CHUNK_HEADS]
            grown_cols[c] = grown[:, c * CHUNK_HEADS : (c + 1) * CHUNK_HEADS]
            carry_cols[c] = carry[:, c * CHUNK_HEADS : (c + 1) * CHUNK_HEADS]
        cum_rows[...] = cum.T
        step_rows[...] = step.T

    @pl.when(i % GROUP_CHUNKS == 0)
    def _():
        b_part = convolved(xb_ref, tailb_ref, wb_ref, bb_ref).astype(jnp.bfloat16)
        c_part = convolved(xc_ref, tailc_ref, wc_ref, bc_ref).astype(jnp.bfloat16)
        b_state[...] = b_part
        c_out_ref[...] = c_part
        both = lax.dot_general(c_part, b_part, (((1,), (1,)), ((), ())), preferred_element_type=jnp.float32)
        scores[...] = jnp.where(t_of >= s_of, both, 0.0)

    x = convolved(x_ref, tail_ref, w_ref, b_ref).astype(jnp.bfloat16)
    x32 = x.astype(jnp.float32)
    first = pl.multiple_of(i * CHUNK_HEADS, CHUNK_HEADS)
    cum_r = cum_rows[pl.ds(first, CHUNK_HEADS), :]
    step_r = step_rows[pl.ds(first, CHUNK_HEADS), :]
    cum_c = cum_cols[i]
    carry_c = carry_cols[i]
    grown_c = grown_cols[i]
    low = lax.broadcasted_iota(jnp.int32, (rows, 128), 1) < HEAD_DIM
    zero = jnp.zeros((rows, 128), jnp.bfloat16)
    for pair in range(CHUNK_HEADS // 2):
        mixes = []
        for j in (2 * pair, 2 * pair + 1):
            diff = cum_c[:, j : j + 1] - cum_r[j : j + 1, :]
            mixes.append((scores[...] * jnp.exp(jnp.minimum(diff, 0.0)) * step_r[j : j + 1, :]).astype(jnp.bfloat16))
        xp = x[:, pair * 128 : (pair + 1) * 128]
        stacked = jnp.concatenate([jnp.where(low, xp, zero), jnp.where(low, zero, xp)], axis=0)
        y = jnp.dot(jnp.concatenate(mixes, axis=1), stacked, preferred_element_type=jnp.float32)
        cols = slice(pair * 128, (pair + 1) * 128)
        y_ref[:, cols] = y + skip_ref[:, cols] * x32[:, cols]
        growth_ref[:, cols] = jnp.where(low, grown_c[:, 2 * pair : 2 * pair + 1], grown_c[:, 2 * pair + 1 : 2 * pair + 2])
        weight = jnp.where(low, carry_c[:, 2 * pair : 2 * pair + 1], carry_c[:, 2 * pair + 1 : 2 * pair + 2])
        carried = (weight * x32[:, cols]).astype(jnp.bfloat16)
        fresh_ref[:, cols] = lax.dot_general(
            b_state[...], carried, (((0,), (0,)), ((), ())), preferred_element_type=jnp.float32
        )


def local_part(base, count, xbc, tail, conv_weight, conv_bias, dt_raw, dt_bias, a_log, skip):
    rows = xbc.shape[0]
    bias = conv_bias[None, :]
    first_b = INNER // 128

    def blocks(height):
        return [
            pl.BlockSpec((height, CHUNK), lambda i: (0, base + i)),
            pl.BlockSpec((height, 128), lambda i: (0, first_b + (base + i) // GROUP_CHUNKS)),
            pl.BlockSpec((height, 128), lambda i: (0, first_b + GROUPS + (base + i) // GROUP_CHUNKS)),
        ]

    whole = lambda *shape: pl.BlockSpec(shape, lambda i: (0, 0))
    return pl.pallas_call(
        functools.partial(local_kernel, base=base),
        grid=(count,),
        out_shape=(
            pltpu.HBM((rows, count * CHUNK), jnp.float32),
            pltpu.HBM((NST, count * CHUNK), jnp.float32),
            pltpu.HBM((rows, count // GROUP_CHUNKS * NST), jnp.bfloat16),
            pltpu.HBM((rows, count * CHUNK), jnp.float32),
        ),
        in_specs=blocks(rows) + blocks(8) + blocks(4) + blocks(1)
        + [whole(rows, HEADS), whole(1, HEADS), whole(1, HEADS), pl.BlockSpec((1, CHUNK), lambda i: (0, base + i))],
        out_specs=(
            pl.BlockSpec((rows, CHUNK), lambda i: (0, i)),
            pl.BlockSpec((NST, CHUNK), lambda i: (0, i)),
            pl.BlockSpec((rows, NST), lambda i: (0, i // GROUP_CHUNKS)),
            pl.BlockSpec((rows, CHUNK), lambda i: (0, i)),
        ),
        scratch_shapes=[
            pltpu.VMEM((CHUNKS, rows, CHUNK_HEADS), jnp.float32),
            pltpu.VMEM((CHUNKS, rows, CHUNK_HEADS), jnp.float32),
            pltpu.VMEM((HEADS, rows), jnp.float32),
            pltpu.VMEM((HEADS, rows), jnp.float32),
            pltpu.VMEM((CHUNKS, rows, CHUNK_HEADS), jnp.float32),
            pltpu.VMEM((rows, rows), jnp.float32),
            pltpu.VMEM((rows, NST), jnp.bfloat16),
        ],
        compiler_params=pltpu.CompilerParams(vmem_limit_bytes=24 * 1024 * 1024),
        cost_estimate=pl.CostEstimate(flops=1000, bytes_accessed=1000, transcendentals=0),
        name="local_part",
    )(
        xbc, xbc, xbc, tail, tail, tail, conv_weight, conv_weight, conv_weight, bias, bias, bias,
        dt_raw, dt_bias[None, :], a_log[None, :], skip,
    )


def state_kernel(live_ref, start_ref, c_ref, growth_ref, y_ref, fresh_ref, y_out_ref, final_ref, *scratch):
    start_in, growth_in, y_in, fresh_in, y_done, final_done, sems_in, sems_out = scratch
    pieces, _, width = start_ref.shape
    live = live_ref[0] > 0
    into, outof = [], []
    for k in range(pieces):
        here = pl.ds(k * width, width)
        sources = (start_ref.at[k], growth_ref.at[:, here], y_ref.at[:, here], fresh_ref.at[:, here])
        held = (start_in, growth_in, y_in, fresh_in)
        into.append([pltpu.make_async_copy(a, b.at[k], sems_in.at[n, k]) for n, (a, b) in enumerate(zip(sources, held))])
        targets = (y_out_ref.at[:, here], final_ref.at[0, :, here])
        held = (y_done, final_done)
        outof.append([pltpu.make_async_copy(b.at[k], a, sems_out.at[n, k]) for n, (a, b) in enumerate(zip(targets, held))])
    for group in into:
        for copy in group:
            copy.start()
    for k in range(pieces):
        for copy in into[k]:
            copy.wait()
        first = k * GROUPS // pieces * NST
        start = start_in[k]
        start = jnp.where(live, start, jnp.zeros_like(start))
        growth = growth_in[k]
        y_state = jnp.dot(c_ref[:, first : first + NST], start, preferred_element_type=jnp.float32)
        y_done[k] = (y_in[k] + growth * y_state).astype(jnp.bfloat16)
        kept = growth[SPAN - 1 :, :] * start.astype(jnp.float32)
        final_done[k] = (kept + fresh_in[k]).astype(jnp.bfloat16)
        for copy in outof[k]:
            copy.start()
    for group in outof:
        for copy in group:
            copy.wait()


def state_part(live, start, c_part, growth, y_local, fresh):
    pieces, _, width = start.shape
    rows = y_local.shape[0]
    vmem = pl.BlockSpec(memory_space=pltpu.VMEM)
    hbm = pl.BlockSpec(memory_space=pl.ANY)
    return pl.pallas_call(
        state_kernel,
        out_shape=(
            jax.ShapeDtypeStruct((rows, INNER), jnp.bfloat16),
            jax.ShapeDtypeStruct((1, NST, INNER), jnp.bfloat16),
        ),
        in_specs=[pl.BlockSpec(memory_space=pltpu.SMEM), hbm, vmem, hbm, hbm, hbm],
        out_specs=(hbm, hbm),
        scratch_shapes=[
            pltpu.VMEM((pieces, NST, width), jnp.bfloat16),
            pltpu.VMEM((pieces, rows, width), jnp.float32),
            pltpu.VMEM((pieces, rows, width), jnp.float32),
            pltpu.VMEM((pieces, NST, width), jnp.float32),
            pltpu.VMEM((pieces, rows, width), jnp.bfloat16),
            pltpu.VMEM((pieces, NST, width), jnp.bfloat16),
            pltpu.SemaphoreType.DMA((4, pieces)),
            pltpu.SemaphoreType.DMA((2, pieces)),
        ],
        compiler_params=pltpu.CompilerParams(vmem_limit_bytes=56 * 1024 * 1024),
        cost_estimate=pl.CostEstimate(flops=2 * 134_000_000, bytes_accessed=18_000_000, transcendentals=0),
        name="state_part",
    )(live, start, c_part, growth, y_local, fresh)


def local(
    xbc, dt_raw, conv_weight, conv_bias, dt_bias, a_log, d_skip, cache_states, cache_tails,
    hit_owner, hit_slot, hit_spans, request_of,
):
    pieces = hit_owner.shape[0]
    swap = lambda array, bits: lax.ppermute(array, "req", [(i, i ^ bits) for i in range(pieces)])
    device = lax.axis_index("req").astype(jnp.int32)
    place = device[None]
    own_tail = served_tail(place, hit_owner, hit_slot, cache_tails)
    column = [own_tail] + [swap(own_tail, k) for k in range(LINES, pieces, LINES)]
    packed = pack(place, hit_owner, hit_slot, request_of, cache_states, pieces)
    packed, column = lax.optimization_barrier((packed, column))
    parts = lax.all_to_all(packed, "req", split_axis=0, concat_axis=0, tiled=True)
    chosen, wanted, offered = choose(place, parts, column)
    start = lax.all_to_all(chosen, "req", split_axis=0, concat_axis=0, tiled=True)

    live = (hit_spans[request_of[0]] > 0).astype(jnp.int32)
    offered = [offered[0]] + [swap(offered[k], k) for k in range(1, LINES)]
    tail = lax.select_n(lax.bitwise_xor(hit_owner[request_of[0]], device) % LINES, *offered)
    tail = jnp.where(live > 0, tail, jnp.zeros_like(tail)).astype(jnp.float32)
    tail = jnp.pad(tail, ((8 - tail.shape[0], 0), (0, 0)))

    skip = jnp.repeat(d_skip, HEAD_DIM)[None, :]
    y_local, fresh, c_part, growth = local_part(0, CHUNKS, xbc, tail, conv_weight, conv_bias, dt_raw, dt_bias, a_log, skip)
    return state_part(live[None], start, c_part, growth, y_local, fresh)


def solution(mesh):
    in_specs = (
        P(("grp", "req"), None),
        P(("grp", "req"), None),
        P(),
        P(),
        P(),
        P(),
        P(),
        P(("grp", "req"), None, None),
        P(("grp", "req"), None, None),
        P("grp"),
        P("grp"),
        P("grp"),
        P(("grp", "req")),
    )
    out_specs = (P(("grp", "req"), None), P(("grp", "req"), None, None))
    return jax.shard_map(local, mesh=mesh, in_specs=in_specs, out_specs=out_specs, check_vma=False)
```

```python
import functools

import jax
import jax.numpy as jnp
from jax import lax
from jax.experimental import pallas as pl
from jax.experimental.pallas import tpu as pltpu
from jax.sharding import PartitionSpec as P

HEADS = 128
HEAD_DIM = 64
GROUPS = 4
NST = 128
INNER = 8192
SPAN = 128
PER_GROUP = HEADS // GROUPS
CHUNK = 512
CHUNK_HEADS = CHUNK // HEAD_DIM
CHUNKS = INNER // CHUNK
GROUP_CHUNKS = CHUNKS // GROUPS
CHANNELS = INNER + 2 * GROUPS * NST
EARLY = 3
GROUP = INNER // GROUPS
NOTE = 8
SMALL = pl.CostEstimate(flops=1000, bytes_accessed=1000, transcendentals=0)


def served_slot(device, owner_ref, slot_ref):
    served = jnp.int32(0)
    for r in range(owner_ref.shape[0]):
        served = jnp.where(owner_ref[r] == device, jnp.maximum(served, slot_ref[r]), served)
    return served


def piece_shape(pieces):
    width = INNER // pieces
    split = 2 if width >= 256 else 1
    return split, width // split


def pack_kernel(
    device_ref, owner_ref, slot_ref, request_ref, cache_ref, tails_ref, out_ref, held, tail, note, sems_in, sems_out, sem
):
    pieces = held.shape[0]
    split, width = piece_shape(pieces)
    share = (CHANNELS - INNER) // pieces
    served = served_slot(device_ref[0], owner_ref, slot_ref)
    tail_copy = pltpu.make_async_copy(tails_ref.at[served], tail, sem)
    tail_copy.start()
    into, outof = [], []
    for p in range(pieces):
        for k in range(split):
            source = cache_ref.at[served, :, pl.ds((p * split + k) * width, width)]
            into.append(pltpu.make_async_copy(source, held.at[p, pl.ds(k * NST, NST)], sems_in.at[p, k]))
        outof.append(pltpu.make_async_copy(held.at[p], out_ref.at[p], sems_out.at[p]))
    for copy in into:
        copy.start()
    note[...] = jnp.zeros(note.shape, jnp.float32)
    note[7:8, :] = jnp.full((1, width), owner_ref[request_ref[0]].astype(jnp.float32))
    tail_copy.wait()
    last = tail[...].astype(jnp.float32)
    taps = last.shape[0]
    for p in range(pieces):
        for k in range(split):
            first = (p * split + k) * width
            note[k * taps : (k + 1) * taps, :] = last[:, first : first + width]
        first = INNER + p * share
        for r in range(taps):
            note[6:7, r * share : (r + 1) * share] = last[r : r + 1, first : first + share]
        held[p, split * NST :, :] = note[...].astype(jnp.bfloat16)
    for p in range(pieces):
        for k in range(split):
            into[p * split + k].wait()
        outof[p].start()
    for copy in outof:
        copy.wait()


def pack(device, hit_owner, hit_slot, request_of, cache_states, cache_tails, pieces):
    smem = pl.BlockSpec(memory_space=pltpu.SMEM)
    hbm = pl.BlockSpec(memory_space=pl.ANY)
    split, width = piece_shape(pieces)
    shape = (pieces, split * NST + NOTE, width)
    return pl.pallas_call(
        pack_kernel,
        out_shape=jax.ShapeDtypeStruct(shape, jnp.bfloat16),
        in_specs=[smem] * 4 + [hbm, hbm],
        out_specs=hbm,
        scratch_shapes=[
            pltpu.VMEM(shape, jnp.bfloat16),
            pltpu.VMEM(cache_tails.shape[1:], jnp.bfloat16),
            pltpu.VMEM((NOTE, width), jnp.float32),
            pltpu.SemaphoreType.DMA((pieces, split)),
            pltpu.SemaphoreType.DMA((pieces,)),
            pltpu.SemaphoreType.DMA,
        ],
        compiler_params=pltpu.CompilerParams(vmem_limit_bytes=56 * 1024 * 1024),
        cost_estimate=SMALL,
        name="pack",
    )(device, hit_owner, hit_slot, request_of, cache_states, cache_tails)


def choose_kernel(parts_ref, out_ref, held, sems_in, sems_out):
    pieces, rows, _ = held.shape
    into = [pltpu.make_async_copy(parts_ref.at[p], held.at[p], sems_in.at[p]) for p in range(pieces)]
    for copy in into:
        copy.start()
    wanted = []
    for p in range(pieces):
        into[p].wait()
        wanted.append(jnp.max(held[p, rows - NOTE :, :128].astype(jnp.float32)[7:8]).astype(jnp.int32))
    outof = []
    for p in range(pieces):
        outof.append(pltpu.make_async_copy(held.at[wanted[p]], out_ref.at[p], sems_out.at[p]))
        outof[p].start()
    for copy in outof:
        copy.wait()


def choose(parts):
    pieces = parts.shape[0]
    hbm = pl.BlockSpec(memory_space=pl.ANY)
    return pl.pallas_call(
        choose_kernel,
        out_shape=jax.ShapeDtypeStruct(parts.shape, jnp.bfloat16),
        in_specs=[hbm],
        out_specs=hbm,
        scratch_shapes=[
            pltpu.VMEM(parts.shape, jnp.bfloat16),
            pltpu.SemaphoreType.DMA((pieces,)),
            pltpu.SemaphoreType.DMA((pieces,)),
        ],
        compiler_params=pltpu.CompilerParams(vmem_limit_bytes=56 * 1024 * 1024),
        cost_estimate=SMALL,
        name="choose",
    )(parts)


def convolved(extended, weight, bias):
    total = bias + weight[3:4, :] * extended
    for back in range(1, 4):
        total = total + weight[3 - back : 4 - back, :] * pltpu.roll(extended, back, 0)
    return total / (1.0 + jnp.exp(-total))


def local_kernel(
    x_ref, xb_ref, xc_ref, w_ref, wb_ref, wc_ref, b_ref, bb_ref, bc_ref,
    dt_ref, dt_bias_ref, a_log_ref, skip_ref,
    y_ref, fresh_ref, c_out_ref, growth_ref, early_ref, early_carry_ref,
    cum_cols, step_cols, cum_rows, step_rows, carry_cols, scores, b_state,
):
    i = pl.program_id(0)
    rows = SPAN
    t_of = lax.broadcasted_iota(jnp.int32, (rows, rows), 0)
    s_of = lax.broadcasted_iota(jnp.int32, (rows, rows), 1)

    @pl.when(pl.program_id(0) == 0)
    def _():
        v = dt_ref[...] + dt_bias_ref[...]
        step = jnp.maximum(v, 0.0) + jnp.log1p(jnp.exp(-jnp.abs(v)))
        rate = -jnp.exp(a_log_ref[...])
        cum = step * rate
        shift = 1
        while shift < rows:
            cum = cum + jnp.where(t_of >= shift, pltpu.roll(cum, shift, 0), 0.0)
            shift *= 2
        growth_ref[...] = jnp.exp(cum)
        carry = jnp.exp(cum[rows - 1 : rows, :] - cum) * step
        for c in range(CHUNKS):
            cum_cols[c] = cum[:, c * CHUNK_HEADS : (c + 1) * CHUNK_HEADS]
            step_cols[c] = step[:, c * CHUNK_HEADS : (c + 1) * CHUNK_HEADS]
            carry_cols[c] = carry[:, c * CHUNK_HEADS : (c + 1) * CHUNK_HEADS]
        cum_rows[...] = cum.T
        step_rows[...] = step.T

    @pl.when(i % GROUP_CHUNKS == 0)
    def _():
        b_part = convolved(xb_ref[...].astype(jnp.float32), wb_ref, bb_ref[...])
        b_part = jnp.where(t_of >= EARLY, b_part, 0.0).astype(jnp.bfloat16)
        c_part = convolved(xc_ref[...].astype(jnp.float32), wc_ref, bc_ref[...]).astype(jnp.bfloat16)
        b_state[...] = b_part
        c_out_ref[...] = c_part
        both = lax.dot_general(c_part, b_part, (((1,), (1,)), ((), ())), preferred_element_type=jnp.float32)
        scores[...] = jnp.where(t_of >= s_of, both, 0.0)

    x = convolved(x_ref[...].astype(jnp.float32), w_ref, b_ref[...])
    x = jnp.where(lax.broadcasted_iota(jnp.int32, x.shape, 0) >= EARLY, x, 0.0).astype(jnp.bfloat16)
    x32 = x.astype(jnp.float32)
    first = pl.multiple_of(i * CHUNK_HEADS, CHUNK_HEADS)
    cum_r = cum_rows[pl.ds(first, CHUNK_HEADS), :]
    step_r = step_rows[pl.ds(first, CHUNK_HEADS), :]
    cum_c = cum_cols[i]
    carry_c = carry_cols[i]
    low = lax.broadcasted_iota(jnp.int32, (rows, 128), 1) < HEAD_DIM
    zero = jnp.zeros((rows, 128), jnp.bfloat16)
    step_c = step_cols[i]
    t_col = lax.broadcasted_iota(jnp.int32, (rows, CHUNK_HEADS), 0)
    early = []
    for s in range(EARLY):
        decay = jnp.exp(jnp.minimum(cum_c - cum_c[s : s + 1, :], 0.0)) * step_c[s : s + 1, :]
        early.append(jnp.where(t_col >= s, decay, 0.0))
    early = jnp.concatenate(early + [jnp.zeros((rows, CHUNK_HEADS), jnp.float32)], axis=1)
    for c in range(GROUP_CHUNKS):

        @pl.when(i % GROUP_CHUNKS == c)
        def _(c=c):
            early_ref[0, :, c * 4 * CHUNK_HEADS : (c + 1) * 4 * CHUNK_HEADS] = early

    for pair in range(CHUNK_HEADS // 2):
        mixes = []
        for j in (2 * pair, 2 * pair + 1):
            diff = cum_c[:, j : j + 1] - cum_r[j : j + 1, :]
            mixes.append((scores[...] * jnp.exp(jnp.minimum(diff, 0.0)) * step_r[j : j + 1, :]).astype(jnp.bfloat16))
        xp = x[:, pair * 128 : (pair + 1) * 128]
        stacked = jnp.concatenate([jnp.where(low, xp, zero), jnp.where(low, zero, xp)], axis=0)
        y = jnp.dot(jnp.concatenate(mixes, axis=1), stacked, preferred_element_type=jnp.float32)
        cols = slice(pair * 128, (pair + 1) * 128)
        y_ref[:, cols] = y + skip_ref[:, cols] * x32[:, cols]
        weight = jnp.where(low, carry_c[:, 2 * pair : 2 * pair + 1], carry_c[:, 2 * pair + 1 : 2 * pair + 2])
        early_carry_ref[:, cols] = weight[:8]
        carried = (weight * x32[:, cols]).astype(jnp.bfloat16)
        fresh_ref[:, cols] = lax.dot_general(
            b_state[...], carried, (((0,), (0,)), ((), ())), preferred_element_type=jnp.float32
        )


def local_part(xbc, conv_weight, conv_bias, dt_raw, dt_bias, a_log, skip):
    rows = xbc.shape[0]
    bias = conv_bias[None, :]
    first_b = INNER // 128

    def blocks(height):
        return [
            pl.BlockSpec((height, CHUNK), lambda i: (0, i)),
            pl.BlockSpec((height, 128), lambda i: (0, first_b + i // GROUP_CHUNKS)),
            pl.BlockSpec((height, 128), lambda i: (0, first_b + GROUPS + i // GROUP_CHUNKS)),
        ]

    whole = lambda *shape: pl.BlockSpec(shape, lambda i: (0, 0))
    return pl.pallas_call(
        local_kernel,
        grid=(CHUNKS,),
        out_shape=(
            pltpu.HBM((rows, INNER), jnp.float32),
            pltpu.HBM((NST, INNER), jnp.float32),
            pltpu.HBM((rows, GROUPS * NST), jnp.bfloat16),
            pltpu.HBM((rows, HEADS), jnp.float32),
            jax.ShapeDtypeStruct((GROUPS, rows, 128), jnp.float32),
            jax.ShapeDtypeStruct((8, INNER), jnp.float32),
        ),
        in_specs=blocks(rows) + blocks(4) + blocks(1)
        + [whole(rows, HEADS), whole(1, HEADS), whole(1, HEADS), pl.BlockSpec((1, CHUNK), lambda i: (0, i))],
        out_specs=(
            pl.BlockSpec((rows, CHUNK), lambda i: (0, i)),
            pl.BlockSpec((NST, CHUNK), lambda i: (0, i)),
            pl.BlockSpec((rows, NST), lambda i: (0, i // GROUP_CHUNKS)),
            whole(rows, HEADS),
            pl.BlockSpec((1, rows, 128), lambda i: (i // GROUP_CHUNKS, 0, 0)),
            pl.BlockSpec((8, CHUNK), lambda i: (0, i)),
        ),
        scratch_shapes=[
            pltpu.VMEM((CHUNKS, rows, CHUNK_HEADS), jnp.float32),
            pltpu.VMEM((CHUNKS, rows, CHUNK_HEADS), jnp.float32),
            pltpu.VMEM((HEADS, rows), jnp.float32),
            pltpu.VMEM((HEADS, rows), jnp.float32),
            pltpu.VMEM((CHUNKS, rows, CHUNK_HEADS), jnp.float32),
            pltpu.VMEM((rows, rows), jnp.float32),
            pltpu.VMEM((rows, NST), jnp.bfloat16),
        ],
        compiler_params=pltpu.CompilerParams(vmem_limit_bytes=24 * 1024 * 1024),
        cost_estimate=pl.CostEstimate(flops=1000, bytes_accessed=1000, transcendentals=0),
        name="local_part",
    )(
        xbc, xbc, xbc, conv_weight, conv_weight, conv_weight, bias, bias, bias,
        dt_raw, dt_bias[None, :], a_log[None, :], skip,
    )


def state_kernel(
    live_ref, start_ref, xbc_ref, c_hbm, growth_hbm, early_hbm, carry_hbm, w_hbm, bias_hbm, skip_hbm, y_ref, fresh_ref,
    y_out_ref, final_ref,
    raw, x_in, c_ref, growth_ref, early_ref, early_carry_ref, w_ref, bias_ref, skip_ref,
    y_in, fresh_in, y_done, final_done, tail, c_full, sems, sems_raw, sems_in, sems_out,
):
    pieces, height, width = raw.shape
    split = height // NST
    blocks = GROUP // width
    share = (CHANNELS - INNER) // pieces
    live = live_ref[0] > 0
    starts = [pltpu.make_async_copy(start_ref.at[p], raw.at[p], sems_raw.at[p]) for p in range(pieces)]
    small = (
        (xbc_ref.at[pl.ds(0, 16)], x_in), (w_hbm, w_ref), (bias_hbm, bias_ref), (c_hbm, c_ref), (growth_hbm, growth_ref),
        (early_hbm, early_ref), (carry_hbm, early_carry_ref), (skip_hbm, skip_ref),
    )
    small = [pltpu.make_async_copy(a, b, sems.at[n]) for n, (a, b) in enumerate(small)]
    into, outof = [], []
    for g in range(GROUPS):
        columns = pl.ds(g * GROUP, GROUP)
        into.append(
            (
                pltpu.make_async_copy(y_ref.at[:, columns], y_in.at[g], sems_in.at[g, 0]),
                pltpu.make_async_copy(fresh_ref.at[:, columns], fresh_in.at[g], sems_in.at[g, 1]),
            )
        )
        outof += [
            pltpu.make_async_copy(y_done.at[g], y_out_ref.at[:, columns], sems_out.at[g, 0]),
            pltpu.make_async_copy(final_done.at[g], final_ref.at[0, :, columns], sems_out.at[g, 1]),
        ]
    for copy in starts + small:
        copy.start()
    for copies in into:
        for copy in copies:
            copy.start()

    tail[...] = jnp.zeros(tail.shape, jnp.float32)
    for p in range(pieces):
        starts[p].wait()
        note = raw[p, split * NST :, :].astype(jnp.float32)
        note = jnp.where(live, note, 0.0)
        for k in range(split):
            first = (p * split + k) * width
            tail[5:8, first : first + width] = note[k * EARLY : (k + 1) * EARLY, :]
        first = INNER + p * share
        for r in range(EARLY):
            tail[5 + r : 6 + r, first : first + share] = note[6:7, r * share : (r + 1) * share]
    for copy in small:
        copy.wait()

    def early_rows(first, size):
        here = slice(first, first + size)
        extended = jnp.concatenate([tail[:, here], x_in[:, here].astype(jnp.float32)[:8]], axis=0)
        rows = convolved(extended, w_ref[:, here], bias_ref[:, here])[8:]
        rows = jnp.where(lax.broadcasted_iota(jnp.int32, rows.shape, 0) < EARLY, rows, 0.0)
        return rows.astype(jnp.bfloat16).astype(jnp.float32)

    def padded(rows):
        return jnp.concatenate([rows, jnp.zeros_like(rows)], axis=0).astype(jnp.bfloat16)

    b_early = early_rows(INNER, GROUPS * NST)
    c_early = padded(early_rows(INNER + GROUPS * NST, GROUPS * NST))
    c_full[...] = c_ref[...]
    sixteen = lax.broadcasted_iota(jnp.int32, c_early.shape, 0)
    c_full[:16, :] = jnp.where(sixteen < EARLY, c_early, c_ref[:16, :])

    low = lax.broadcasted_iota(jnp.int32, (SPAN, 128), 1) < HEAD_DIM
    row = lax.broadcasted_iota(jnp.int32, (128, 128), 0)
    token = row % (4 * CHUNK_HEADS) // CHUNK_HEADS
    wide_row = lax.broadcasted_iota(jnp.int32, (128, width), 0)
    wide_token = wide_row % (4 * CHUNK_HEADS) // CHUNK_HEADS
    wide_head = wide_row // (4 * CHUNK_HEADS) * CHUNK_HEADS + wide_row % CHUNK_HEADS
    lane_head = lax.broadcasted_iota(jnp.int32, (128, width), 1) // HEAD_DIM

    def by_token(of, rows):
        return jnp.where(of == 0, rows[0:1], jnp.where(of == 1, rows[1:2], jnp.where(of == 2, rows[2:3], 0.0)))

    for g in range(GROUPS):
        c_group = c_full[:, g * NST : (g + 1) * NST]
        b_group = b_early[:, g * NST : (g + 1) * NST]
        both = lax.dot_general(
            c_group, by_token(token, b_group).astype(jnp.bfloat16), (((1,), (1,)), ((), ())),
            preferred_element_type=jnp.float32,
        )
        mixing = (both * early_ref[g]).astype(jnp.bfloat16)
        b_group = padded(b_group)
        for copy in into[g]:
            copy.wait()
        for n in range(blocks):
            first = g * GROUP + n * width
            here, inside = slice(first, first + width), slice(n * width, (n + 1) * width)
            x_early = early_rows(first, width)
            base = first // width % split * NST
            start = raw[first // (split * width), base : base + NST, :]
            start = jnp.where(live, start, jnp.zeros_like(start))
            y_state = jnp.dot(c_group, start, preferred_element_type=jnp.float32)
            heads = range(first // HEAD_DIM, (first + width) // HEAD_DIM, 2)
            growth = [jnp.where(low, growth_ref[:, h : h + 1], growth_ref[:, h + 1 : h + 2]) for h in heads]
            growth = jnp.concatenate(growth, axis=1) if len(growth) > 1 else growth[0]
            mine = wide_head == lane_head + n * (width // HEAD_DIM)
            inputs = jnp.where(mine, by_token(wide_token, x_early), 0.0).astype(jnp.bfloat16)
            y = y_in[g, :, inside] + growth * y_state + jnp.dot(mixing, inputs, preferred_element_type=jnp.float32)
            skipped = y[:8] + skip_ref[:, here] * x_early
            y_done[g, :, inside] = jnp.concatenate([skipped, y[8:]], axis=0).astype(jnp.bfloat16)
            carried = padded(early_carry_ref[:, here] * x_early)
            fresh = fresh_in[g, :, inside] + lax.dot_general(
                b_group, carried, (((0,), (0,)), ((), ())), preferred_element_type=jnp.float32
            )
            kept = growth[SPAN - 1 :, :] * start.astype(jnp.float32)
            final_done[g, :, inside] = (kept + fresh).astype(jnp.bfloat16)
        outof[2 * g].start()
        outof[2 * g + 1].start()
    for copy in outof:
        copy.wait()


def state_part(live, start, xbc, local_results, conv_weight, conv_bias, skip):
    y_local, fresh, c_part, growth, early, early_carry = local_results
    rows = y_local.shape[0]
    hbm = pl.BlockSpec(memory_space=pl.ANY)
    return pl.pallas_call(
        state_kernel,
        out_shape=(
            jax.ShapeDtypeStruct((rows, INNER), jnp.bfloat16),
            jax.ShapeDtypeStruct((1, NST, INNER), jnp.bfloat16),
        ),
        in_specs=[pl.BlockSpec(memory_space=pltpu.SMEM)] + [hbm] * 11,
        out_specs=(hbm, hbm),
        scratch_shapes=[
            pltpu.VMEM(start.shape, jnp.bfloat16),
            pltpu.VMEM((16, CHANNELS), jnp.bfloat16),
            pltpu.VMEM(c_part.shape, c_part.dtype),
            pltpu.VMEM(growth.shape, growth.dtype),
            pltpu.VMEM(early.shape, early.dtype),
            pltpu.VMEM(early_carry.shape, early_carry.dtype),
            pltpu.VMEM(conv_weight.shape, conv_weight.dtype),
            pltpu.VMEM((1, CHANNELS), jnp.float32),
            pltpu.VMEM((1, INNER), jnp.float32),
            pltpu.VMEM((GROUPS, rows, GROUP), jnp.float32),
            pltpu.VMEM((GROUPS, NST, GROUP), jnp.float32),
            pltpu.VMEM((GROUPS, rows, GROUP), jnp.bfloat16),
            pltpu.VMEM((GROUPS, NST, GROUP), jnp.bfloat16),
            pltpu.VMEM((8, CHANNELS), jnp.float32),
            pltpu.VMEM((rows, GROUPS * NST), jnp.bfloat16),
            pltpu.SemaphoreType.DMA((8,)),
            pltpu.SemaphoreType.DMA((start.shape[0],)),
            pltpu.SemaphoreType.DMA((GROUPS, 2)),
            pltpu.SemaphoreType.DMA((GROUPS, 2)),
        ],
        compiler_params=pltpu.CompilerParams(vmem_limit_bytes=52 * 1024 * 1024),
        cost_estimate=pl.CostEstimate(flops=3 * 134_000_000, bytes_accessed=15_000_000, transcendentals=0),
        name="state_part",
    )(live, start, xbc, c_part, growth, early, early_carry, conv_weight, conv_bias[None, :], skip, y_local, fresh)


def local(
    xbc, dt_raw, conv_weight, conv_bias, dt_bias, a_log, d_skip, cache_states, cache_tails,
    hit_owner, hit_slot, hit_spans, request_of,
):
    pieces = hit_owner.shape[0]
    place = lax.axis_index("req").astype(jnp.int32)[None]
    packed = pack(place, hit_owner, hit_slot, request_of, cache_states, cache_tails, pieces)
    parts = lax.all_to_all(packed, "req", split_axis=0, concat_axis=0, tiled=True)
    start = lax.all_to_all(choose(parts), "req", split_axis=0, concat_axis=0, tiled=True)

    live = (hit_spans[request_of[0]] > 0).astype(jnp.int32)[None]
    skip = jnp.repeat(d_skip, HEAD_DIM)[None, :]
    without = local_part(xbc, conv_weight, conv_bias, dt_raw, dt_bias, a_log, skip)
    return state_part(live, start, xbc, without, conv_weight, conv_bias, skip)


def solution(mesh):
    in_specs = (
        P(("grp", "req"), None),
        P(("grp", "req"), None),
        P(),
        P(),
        P(),
        P(),
        P(),
        P(("grp", "req"), None, None),
        P(("grp", "req"), None, None),
        P("grp"),
        P("grp"),
        P("grp"),
        P(("grp", "req")),
    )
    out_specs = (P(("grp", "req"), None), P(("grp", "req"), None, None))
    return jax.shard_map(local, mesh=mesh, in_specs=in_specs, out_specs=out_specs, check_vma=False)
```

```python
import functools

import jax
import jax.numpy as jnp
from jax import lax
from jax.experimental import pallas as pl
from jax.experimental.pallas import tpu as pltpu
from jax.sharding import PartitionSpec as P

HEADS = 128
HEAD_DIM = 64
GROUPS = 4
NST = 128
INNER = 8192
SPAN = 128
PER_GROUP = HEADS // GROUPS
CHUNK = 512
CHUNK_HEADS = CHUNK // HEAD_DIM
CHUNKS = INNER // CHUNK
GROUP_CHUNKS = CHUNKS // GROUPS
CHANNELS = INNER + 2 * GROUPS * NST
EARLY = 3
GROUP = INNER // GROUPS
NOTE = 8
SMALL = pl.CostEstimate(flops=1000, bytes_accessed=1000, transcendentals=0)


def served_slot(device, owner_ref, slot_ref):
    served = jnp.int32(0)
    for r in range(owner_ref.shape[0]):
        served = jnp.where(owner_ref[r] == device, jnp.maximum(served, slot_ref[r]), served)
    return served


def piece_shape(pieces):
    width = INNER // pieces
    split = 2 if width >= 256 else 1
    return split, width // split


def pack_kernel(
    device_ref, owner_ref, slot_ref, request_ref, cache_ref, tails_ref, held, tail, note, sems_in, sem
):
    pieces = held.shape[0]
    split, width = piece_shape(pieces)
    share = (CHANNELS - INNER) // pieces
    served = served_slot(device_ref[0], owner_ref, slot_ref)
    tail_copy = pltpu.make_async_copy(tails_ref.at[served], tail, sem)
    tail_copy.start()
    into = []
    for p in range(pieces):
        for k in range(split):
            source = cache_ref.at[served, :, pl.ds((p * split + k) * width, width)]
            into.append(pltpu.make_async_copy(source, held.at[p, pl.ds(k * NST, NST)], sems_in.at[p, k]))
    for copy in into:
        copy.start()
    note[...] = jnp.zeros(note.shape, jnp.float32)
    note[7:8, :] = jnp.full((1, width), owner_ref[request_ref[0]].astype(jnp.float32))
    tail_copy.wait()
    last = tail[...].astype(jnp.float32)
    taps = last.shape[0]
    for p in range(pieces):
        for k in range(split):
            first = (p * split + k) * width
            note[k * taps : (k + 1) * taps, :] = last[:, first : first + width]
        first = INNER + p * share
        for r in range(taps):
            note[6:7, r * share : (r + 1) * share] = last[r : r + 1, first : first + share]
        held[p, split * NST :, :] = note[...].astype(jnp.bfloat16)
    for copy in into:
        copy.wait()


def pack(device, hit_owner, hit_slot, request_of, cache_states, cache_tails, pieces):
    smem = pl.BlockSpec(memory_space=pltpu.SMEM)
    hbm = pl.BlockSpec(memory_space=pl.ANY)
    split, width = piece_shape(pieces)
    shape = (pieces, split * NST + NOTE, width)
    return pl.pallas_call(
        pack_kernel,
        out_shape=pltpu.VMEM(shape, jnp.bfloat16),
        in_specs=[smem] * 4 + [hbm, hbm],
        out_specs=pl.BlockSpec(memory_space=pltpu.VMEM),
        scratch_shapes=[
            pltpu.VMEM(cache_tails.shape[1:], jnp.bfloat16),
            pltpu.VMEM((NOTE, width), jnp.float32),
            pltpu.SemaphoreType.DMA((pieces, split)),
            pltpu.SemaphoreType.DMA,
        ],
        compiler_params=pltpu.CompilerParams(vmem_limit_bytes=56 * 1024 * 1024),
        cost_estimate=SMALL,
        name="pack",
    )(device, hit_owner, hit_slot, request_of, cache_states, cache_tails)


def choose_kernel(held, out_ref, sems_out):
    pieces, rows, _ = held.shape
    wanted = []
    for p in range(pieces):
        wanted.append(jnp.max(held[p, rows - NOTE :, :128].astype(jnp.float32)[7:8]).astype(jnp.int32))
    outof = []
    for p in range(pieces):
        outof.append(pltpu.make_async_copy(held.at[wanted[p]], out_ref.at[p], sems_out.at[p]))
        outof[p].start()
    for copy in outof:
        copy.wait()


def choose(parts):
    pieces = parts.shape[0]
    hbm = pl.BlockSpec(memory_space=pl.ANY)
    return pl.pallas_call(
        choose_kernel,
        out_shape=jax.ShapeDtypeStruct(parts.shape, jnp.bfloat16),
        in_specs=[pl.BlockSpec(memory_space=pltpu.VMEM)],
        out_specs=hbm,
        scratch_shapes=[
            pltpu.SemaphoreType.DMA((pieces,)),
        ],
        compiler_params=pltpu.CompilerParams(vmem_limit_bytes=16 * 1024 * 1024),
        cost_estimate=SMALL,
        name="choose",
    )(parts)


def convolved(extended, weight, bias):
    total = bias + weight[3:4, :] * extended
    for back in range(1, 4):
        total = total + weight[3 - back : 4 - back, :] * pltpu.roll(extended, back, 0)
    return total / (1.0 + jnp.exp(-total))


def local_kernel(
    x_ref, xb_ref, xc_ref, w_ref, wb_ref, wc_ref, b_ref, bb_ref, bc_ref,
    dt_ref, dt_bias_ref, a_log_ref, skip_ref,
    y_ref, fresh_ref, c_out_ref, growth_ref, early_ref, early_carry_ref,
    cum_cols, step_cols, cum_rows, step_rows, carry_cols, scores, b_state,
):
    i = pl.program_id(0)
    rows = SPAN
    t_of = lax.broadcasted_iota(jnp.int32, (rows, rows), 0)
    s_of = lax.broadcasted_iota(jnp.int32, (rows, rows), 1)

    @pl.when(pl.program_id(0) == 0)
    def _():
        v = dt_ref[...] + dt_bias_ref[...]
        step = jnp.maximum(v, 0.0) + jnp.log1p(jnp.exp(-jnp.abs(v)))
        rate = -jnp.exp(a_log_ref[...])
        cum = step * rate
        shift = 1
        while shift < rows:
            cum = cum + jnp.where(t_of >= shift, pltpu.roll(cum, shift, 0), 0.0)
            shift *= 2
        growth_ref[...] = jnp.exp(cum)
        carry = jnp.exp(cum[rows - 1 : rows, :] - cum) * step
        for c in range(CHUNKS):
            cum_cols[c] = cum[:, c * CHUNK_HEADS : (c + 1) * CHUNK_HEADS]
            step_cols[c] = step[:, c * CHUNK_HEADS : (c + 1) * CHUNK_HEADS]
            carry_cols[c] = carry[:, c * CHUNK_HEADS : (c + 1) * CHUNK_HEADS]
        cum_rows[...] = cum.T
        step_rows[...] = step.T

    @pl.when(i % GROUP_CHUNKS == 0)
    def _():
        b_part = convolved(xb_ref[...].astype(jnp.float32), wb_ref, bb_ref[...])
        b_part = jnp.where(t_of >= EARLY, b_part, 0.0).astype(jnp.bfloat16)
        c_part = convolved(xc_ref[...].astype(jnp.float32), wc_ref, bc_ref[...]).astype(jnp.bfloat16)
        b_state[...] = b_part
        c_out_ref[...] = c_part
        both = lax.dot_general(c_part, b_part, (((1,), (1,)), ((), ())), preferred_element_type=jnp.float32)
        scores[...] = jnp.where(t_of >= s_of, both, 0.0)

    x = convolved(x_ref[...].astype(jnp.float32), w_ref, b_ref[...])
    x = jnp.where(lax.broadcasted_iota(jnp.int32, x.shape, 0) >= EARLY, x, 0.0).astype(jnp.bfloat16)
    x32 = x.astype(jnp.float32)
    first = pl.multiple_of(i * CHUNK_HEADS, CHUNK_HEADS)
    cum_r = cum_rows[pl.ds(first, CHUNK_HEADS), :]
    step_r = step_rows[pl.ds(first, CHUNK_HEADS), :]
    cum_c = cum_cols[i]
    carry_c = carry_cols[i]
    low = lax.broadcasted_iota(jnp.int32, (rows, 128), 1) < HEAD_DIM
    zero = jnp.zeros((rows, 128), jnp.bfloat16)
    step_c = step_cols[i]
    t_col = lax.broadcasted_iota(jnp.int32, (rows, CHUNK_HEADS), 0)
    early = []
    for s in range(EARLY):
        decay = jnp.exp(jnp.minimum(cum_c - cum_c[s : s + 1, :], 0.0)) * step_c[s : s + 1, :]
        early.append(jnp.where(t_col >= s, decay, 0.0))
    early = jnp.concatenate(early + [jnp.zeros((rows, CHUNK_HEADS), jnp.float32)], axis=1)
    for c in range(GROUP_CHUNKS):

        @pl.when(i % GROUP_CHUNKS == c)
        def _(c=c):
            early_ref[0, :, c * 4 * CHUNK_HEADS : (c + 1) * 4 * CHUNK_HEADS] = early

    for pair in range(CHUNK_HEADS // 2):
        mixes = []
        for j in (2 * pair, 2 * pair + 1):
            diff = cum_c[:, j : j + 1] - cum_r[j : j + 1, :]
            mixes.append((scores[...] * jnp.exp(jnp.minimum(diff, 0.0)) * step_r[j : j + 1, :]).astype(jnp.bfloat16))
        xp = x[:, pair * 128 : (pair + 1) * 128]
        stacked = jnp.concatenate([jnp.where(low, xp, zero), jnp.where(low, zero, xp)], axis=0)
        y = jnp.dot(jnp.concatenate(mixes, axis=1), stacked, preferred_element_type=jnp.float32)
        cols = slice(pair * 128, (pair + 1) * 128)
        y_ref[:, cols] = y + skip_ref[:, cols] * x32[:, cols]
        weight = jnp.where(low, carry_c[:, 2 * pair : 2 * pair + 1], carry_c[:, 2 * pair + 1 : 2 * pair + 2])
        early_carry_ref[:, cols] = weight[:8]
        carried = (weight * x32[:, cols]).astype(jnp.bfloat16)
        fresh_ref[:, cols] = lax.dot_general(
            b_state[...], carried, (((0,), (0,)), ((), ())), preferred_element_type=jnp.float32
        )


def local_part(xbc, conv_weight, conv_bias, dt_raw, dt_bias, a_log, skip):
    rows = xbc.shape[0]
    bias = conv_bias[None, :]
    first_b = INNER // 128

    def blocks(height):
        return [
            pl.BlockSpec((height, CHUNK), lambda i: (0, i)),
            pl.BlockSpec((height, 128), lambda i: (0, first_b + i // GROUP_CHUNKS)),
            pl.BlockSpec((height, 128), lambda i: (0, first_b + GROUPS + i // GROUP_CHUNKS)),
        ]

    whole = lambda *shape: pl.BlockSpec(shape, lambda i: (0, 0))
    return pl.pallas_call(
        local_kernel,
        grid=(CHUNKS,),
        out_shape=(
            pltpu.HBM((rows, INNER), jnp.float32),
            pltpu.HBM((NST, INNER), jnp.float32),
            pltpu.HBM((rows, GROUPS * NST), jnp.bfloat16),
            pltpu.HBM((rows, HEADS), jnp.float32),
            pltpu.HBM((GROUPS, rows, 128), jnp.float32),
            pltpu.HBM((8, INNER), jnp.float32),
        ),
        in_specs=blocks(rows) + blocks(4) + blocks(1)
        + [whole(rows, HEADS), whole(1, HEADS), whole(1, HEADS), pl.BlockSpec((1, CHUNK), lambda i: (0, i))],
        out_specs=(
            pl.BlockSpec((rows, CHUNK), lambda i: (0, i)),
            pl.BlockSpec((NST, CHUNK), lambda i: (0, i)),
            pl.BlockSpec((rows, NST), lambda i: (0, i // GROUP_CHUNKS)),
            whole(rows, HEADS),
            pl.BlockSpec((1, rows, 128), lambda i: (i // GROUP_CHUNKS, 0, 0)),
            pl.BlockSpec((8, CHUNK), lambda i: (0, i)),
        ),
        scratch_shapes=[
            pltpu.VMEM((CHUNKS, rows, CHUNK_HEADS), jnp.float32),
            pltpu.VMEM((CHUNKS, rows, CHUNK_HEADS), jnp.float32),
            pltpu.VMEM((HEADS, rows), jnp.float32),
            pltpu.VMEM((HEADS, rows), jnp.float32),
            pltpu.VMEM((CHUNKS, rows, CHUNK_HEADS), jnp.float32),
            pltpu.VMEM((rows, rows), jnp.float32),
            pltpu.VMEM((rows, NST), jnp.bfloat16),
        ],
        compiler_params=pltpu.CompilerParams(vmem_limit_bytes=24 * 1024 * 1024),
        cost_estimate=pl.CostEstimate(flops=1000, bytes_accessed=1000, transcendentals=0),
        name="local_part",
    )(
        xbc, xbc, xbc, conv_weight, conv_weight, conv_weight, bias, bias, bias,
        dt_raw, dt_bias[None, :], a_log[None, :], skip,
    )


def state_kernel(
    live_ref, start_ref, xbc_ref, c_hbm, growth_hbm, early_hbm, carry_hbm, w_hbm, bias_hbm, skip_hbm, y_ref, fresh_ref,
    y_out_ref, final_ref,
    raw, x_in, c_ref, growth_ref, early_ref, early_carry_ref, w_ref, bias_ref, skip_ref,
    y_in, fresh_in, y_done, final_done, tail, c_full, sems, sems_raw, sems_in, sems_out,
):
    pieces, height, width = raw.shape
    split = height // NST
    blocks = GROUP // width
    share = (CHANNELS - INNER) // pieces
    live = live_ref[0] > 0
    starts = [pltpu.make_async_copy(start_ref.at[p], raw.at[p], sems_raw.at[p]) for p in range(pieces)]
    small = (
        (xbc_ref.at[pl.ds(0, 16)], x_in), (w_hbm, w_ref), (bias_hbm, bias_ref), (c_hbm, c_ref), (growth_hbm, growth_ref),
        (early_hbm, early_ref), (carry_hbm, early_carry_ref), (skip_hbm, skip_ref),
    )
    small = [pltpu.make_async_copy(a, b, sems.at[n]) for n, (a, b) in enumerate(small)]
    into, outof = [], []
    for g in range(GROUPS):
        columns = pl.ds(g * GROUP, GROUP)
        into.append(
            (
                pltpu.make_async_copy(y_ref.at[:, columns], y_in.at[g], sems_in.at[g, 0]),
                pltpu.make_async_copy(fresh_ref.at[:, columns], fresh_in.at[g], sems_in.at[g, 1]),
            )
        )
        outof += [
            pltpu.make_async_copy(y_done.at[g], y_out_ref.at[:, columns], sems_out.at[g, 0]),
            pltpu.make_async_copy(final_done.at[g], final_ref.at[0, :, columns], sems_out.at[g, 1]),
        ]
    for copy in starts + small:
        copy.start()
    for copies in into:
        for copy in copies:
            copy.start()

    tail[...] = jnp.zeros(tail.shape, jnp.float32)
    for p in range(pieces):
        starts[p].wait()
        note = raw[p, split * NST :, :].astype(jnp.float32)
        note = jnp.where(live, note, 0.0)
        for k in range(split):
            first = (p * split + k) * width
            tail[5:8, first : first + width] = note[k * EARLY : (k + 1) * EARLY, :]
        first = INNER + p * share
        for r in range(EARLY):
            tail[5 + r : 6 + r, first : first + share] = note[6:7, r * share : (r + 1) * share]
    for copy in small:
        copy.wait()

    def early_rows(first, size):
        here = slice(first, first + size)
        extended = jnp.concatenate([tail[:, here], x_in[:, here].astype(jnp.float32)[:8]], axis=0)
        rows = convolved(extended, w_ref[:, here], bias_ref[:, here])[8:]
        rows = jnp.where(lax.broadcasted_iota(jnp.int32, rows.shape, 0) < EARLY, rows, 0.0)
        return rows.astype(jnp.bfloat16).astype(jnp.float32)

    def padded(rows):
        return jnp.concatenate([rows, jnp.zeros_like(rows)], axis=0).astype(jnp.bfloat16)

    b_early = early_rows(INNER, GROUPS * NST)
    c_early = padded(early_rows(INNER + GROUPS * NST, GROUPS * NST))
    c_full[...] = c_ref[...]
    sixteen = lax.broadcasted_iota(jnp.int32, c_early.shape, 0)
    c_full[:16, :] = jnp.where(sixteen < EARLY, c_early, c_ref[:16, :])

    grown = jnp.where(live, growth_ref[...], 0.0)
    group_head = lax.broadcasted_iota(jnp.int32, (4 * PER_GROUP, width), 0)
    lane_of = lax.broadcasted_iota(jnp.int32, (4 * PER_GROUP, width), 1) // HEAD_DIM
    spreads = []
    for n in range(blocks):
        mine = (group_head % PER_GROUP == lane_of + n * (width // HEAD_DIM)) & (group_head < 3 * PER_GROUP)
        spreads.append(jnp.where(mine, 1.0, 0.0).astype(jnp.bfloat16))
    row = lax.broadcasted_iota(jnp.int32, (128, 128), 0)
    token = row % (4 * CHUNK_HEADS) // CHUNK_HEADS
    own_head = lax.broadcasted_iota(jnp.int32, (CHUNK_HEADS, width), 0)
    lane_head = lax.broadcasted_iota(jnp.int32, (CHUNK_HEADS, width), 1) // HEAD_DIM

    def by_token(of, rows):
        return jnp.where(of == 0, rows[0:1], jnp.where(of == 1, rows[1:2], jnp.where(of == 2, rows[2:3], 0.0)))

    for g in range(GROUPS):
        c_group = c_full[:, g * NST : (g + 1) * NST]
        b_group = b_early[:, g * NST : (g + 1) * NST]
        both = lax.dot_general(
            c_group, by_token(token, b_group).astype(jnp.bfloat16), (((1,), (1,)), ((), ())),
            preferred_element_type=jnp.float32,
        )
        mixing = (both * early_ref[g]).astype(jnp.bfloat16)
        b_group = padded(b_group)
        rest = grown[:, g * PER_GROUP : (g + 1) * PER_GROUP]
        exact = []
        for _ in range(3):
            exact.append(rest.astype(jnp.bfloat16).astype(jnp.float32))
            rest = rest - exact[-1]
        exact = jnp.concatenate(exact + [jnp.zeros_like(rest)], axis=1).astype(jnp.bfloat16)
        for copy in into[g]:
            copy.wait()
        for n in range(blocks):
            first = g * GROUP + n * width
            here, inside = slice(first, first + width), slice(n * width, (n + 1) * width)
            x_early = early_rows(first, width)
            base = first // width % split * NST
            start = raw[first // (split * width), base : base + NST, :]
            y_state = jnp.dot(c_group, start, preferred_element_type=jnp.float32)
            growth = jnp.dot(exact, spreads[n], preferred_element_type=jnp.float32)
            chunk = n * width // CHUNK
            mine = own_head == lane_head + n * width % CHUNK // HEAD_DIM
            inputs = [jnp.where(mine, x_early[s : s + 1], 0.0) for s in range(EARLY)]
            inputs = jnp.concatenate(inputs + [jnp.zeros_like(inputs[0])], axis=0).astype(jnp.bfloat16)
            factors = mixing[:, chunk * 4 * CHUNK_HEADS : (chunk + 1) * 4 * CHUNK_HEADS]
            y = y_in[g, :, inside] + growth * y_state + jnp.dot(factors, inputs, preferred_element_type=jnp.float32)
            skipped = y[:8] + skip_ref[:, here] * x_early
            y_done[g, :, inside] = jnp.concatenate([skipped, y[8:]], axis=0).astype(jnp.bfloat16)
            carried = padded(early_carry_ref[:, here] * x_early)
            fresh = fresh_in[g, :, inside] + lax.dot_general(
                b_group, carried, (((0,), (0,)), ((), ())), preferred_element_type=jnp.float32
            )
            kept = growth[SPAN - 1 :, :] * start.astype(jnp.float32)
            final_done[g, :, inside] = (kept + fresh).astype(jnp.bfloat16)
        outof[2 * g].start()
        outof[2 * g + 1].start()
    for copy in outof:
        copy.wait()


def state_part(live, start, xbc, local_results, conv_weight, conv_bias, skip):
    y_local, fresh, c_part, growth, early, early_carry = local_results
    rows = y_local.shape[0]
    hbm = pl.BlockSpec(memory_space=pl.ANY)
    return pl.pallas_call(
        state_kernel,
        out_shape=(
            jax.ShapeDtypeStruct((rows, INNER), jnp.bfloat16),
            jax.ShapeDtypeStruct((1, NST, INNER), jnp.bfloat16),
        ),
        in_specs=[pl.BlockSpec(memory_space=pltpu.SMEM)] + [hbm] * 11,
        out_specs=(hbm, hbm),
        scratch_shapes=[
            pltpu.VMEM(start.shape, jnp.bfloat16),
            pltpu.VMEM((16, CHANNELS), jnp.bfloat16),
            pltpu.VMEM(c_part.shape, c_part.dtype),
            pltpu.VMEM(growth.shape, growth.dtype),
            pltpu.VMEM(early.shape, early.dtype),
            pltpu.VMEM(early_carry.shape, early_carry.dtype),
            pltpu.VMEM(conv_weight.shape, conv_weight.dtype),
            pltpu.VMEM((1, CHANNELS), jnp.float32),
            pltpu.VMEM((1, INNER), jnp.float32),
            pltpu.VMEM((GROUPS, rows, GROUP), jnp.float32),
            pltpu.VMEM((GROUPS, NST, GROUP), jnp.float32),
            pltpu.VMEM((GROUPS, rows, GROUP), jnp.bfloat16),
            pltpu.VMEM((GROUPS, NST, GROUP), jnp.bfloat16),
            pltpu.VMEM((8, CHANNELS), jnp.float32),
            pltpu.VMEM((rows, GROUPS * NST), jnp.bfloat16),
            pltpu.SemaphoreType.DMA((8,)),
            pltpu.SemaphoreType.DMA((start.shape[0],)),
            pltpu.SemaphoreType.DMA((GROUPS, 2)),
            pltpu.SemaphoreType.DMA((GROUPS, 2)),
        ],
        compiler_params=pltpu.CompilerParams(vmem_limit_bytes=52 * 1024 * 1024),
        cost_estimate=pl.CostEstimate(flops=3 * 134_000_000, bytes_accessed=15_000_000, transcendentals=0),
        name="state_part",
    )(live, start, xbc, c_part, growth, early, early_carry, conv_weight, conv_bias[None, :], skip, y_local, fresh)


def local(
    xbc, dt_raw, conv_weight, conv_bias, dt_bias, a_log, d_skip, cache_states, cache_tails,
    hit_owner, hit_slot, hit_spans, request_of,
):
    pieces = hit_owner.shape[0]
    place = lax.axis_index("req").astype(jnp.int32)[None]
    packed = pack(place, hit_owner, hit_slot, request_of, cache_states, cache_tails, pieces)
    parts = lax.all_to_all(packed, "req", split_axis=0, concat_axis=0, tiled=True)
    skip = jnp.repeat(d_skip, HEAD_DIM)[None, :]
    without = local_part(xbc, conv_weight, conv_bias, dt_raw, dt_bias, a_log, skip)
    parts, without = lax.optimization_barrier((parts, without))
    start = lax.all_to_all(choose(parts), "req", split_axis=0, concat_axis=0, tiled=True)

    live = (hit_spans[request_of[0]] > 0).astype(jnp.int32)[None]
    return state_part(live, start, xbc, without, conv_weight, conv_bias, skip)


def solution(mesh):
    in_specs = (
        P(("grp", "req"), None),
        P(("grp", "req"), None),
        P(),
        P(),
        P(),
        P(),
        P(),
        P(("grp", "req"), None, None),
        P(("grp", "req"), None, None),
        P("grp"),
        P("grp"),
        P("grp"),
        P(("grp", "req")),
    )
    out_specs = (P(("grp", "req"), None), P(("grp", "req"), None, None))
    return jax.shard_map(local, mesh=mesh, in_specs=in_specs, out_specs=out_specs, check_vma=False)
```

```python
import functools

import jax
import jax.numpy as jnp
from jax import lax
from jax.experimental import pallas as pl
from jax.experimental.pallas import tpu as pltpu
from jax.sharding import PartitionSpec as P

HEADS = 128
HEAD_DIM = 64
GROUPS = 4
NST = 128
INNER = 8192
SPAN = 128
PER_GROUP = HEADS // GROUPS
CHUNK = 512
CHUNK_HEADS = CHUNK // HEAD_DIM
CHUNKS = INNER // CHUNK
GROUP_CHUNKS = CHUNKS // GROUPS
CHANNELS = INNER + 2 * GROUPS * NST
EARLY = 3
GROUP = INNER // GROUPS
NOTE = 8
SMALL = pl.CostEstimate(flops=1000, bytes_accessed=1000, transcendentals=0)


def served_slot(device, owner_ref, slot_ref):
    served = jnp.int32(0)
    for r in range(owner_ref.shape[0]):
        served = jnp.where(owner_ref[r] == device, jnp.maximum(served, slot_ref[r]), served)
    return served


def piece_shape(pieces):
    width = INNER // pieces
    split = 2 if width >= 256 else 1
    return split, width // split


def pack_kernel(
    device_ref, owner_ref, slot_ref, request_ref, cache_ref, tails_ref, held, tail, note, sems_in, sem
):
    pieces = held.shape[0]
    split, width = piece_shape(pieces)
    share = (CHANNELS - INNER) // pieces
    served = served_slot(device_ref[0], owner_ref, slot_ref)
    tail_copy = pltpu.make_async_copy(tails_ref.at[served], tail, sem)
    tail_copy.start()
    into = []
    for p in range(pieces):
        for k in range(split):
            source = cache_ref.at[served, :, pl.ds((p * split + k) * width, width)]
            into.append(pltpu.make_async_copy(source, held.at[p, pl.ds(k * NST, NST)], sems_in.at[p, k]))
    for copy in into:
        copy.start()
    note[...] = jnp.zeros(note.shape, jnp.float32)
    note[7:8, :] = jnp.full((1, width), owner_ref[request_ref[0]].astype(jnp.float32))
    tail_copy.wait()
    last = tail[...].astype(jnp.float32)
    taps = last.shape[0]
    for p in range(pieces):
        for k in range(split):
            first = (p * split + k) * width
            note[k * taps : (k + 1) * taps, :] = last[:, first : first + width]
        first = INNER + p * share
        for r in range(taps):
            note[6:7, r * share : (r + 1) * share] = last[r : r + 1, first : first + share]
        held[p, split * NST :, :] = note[...].astype(jnp.bfloat16)
    for copy in into:
        copy.wait()


def pack(device, hit_owner, hit_slot, request_of, cache_states, cache_tails, pieces):
    smem = pl.BlockSpec(memory_space=pltpu.SMEM)
    hbm = pl.BlockSpec(memory_space=pl.ANY)
    split, width = piece_shape(pieces)
    shape = (pieces, split * NST + NOTE, width)
    return pl.pallas_call(
        pack_kernel,
        out_shape=pltpu.VMEM(shape, jnp.bfloat16),
        in_specs=[smem] * 4 + [hbm, hbm],
        out_specs=pl.BlockSpec(memory_space=pltpu.VMEM),
        scratch_shapes=[
            pltpu.VMEM(cache_tails.shape[1:], jnp.bfloat16),
            pltpu.VMEM((NOTE, width), jnp.float32),
            pltpu.SemaphoreType.DMA((pieces, split)),
            pltpu.SemaphoreType.DMA,
        ],
        compiler_params=pltpu.CompilerParams(vmem_limit_bytes=56 * 1024 * 1024),
        cost_estimate=SMALL,
        name="pack",
    )(device, hit_owner, hit_slot, request_of, cache_states, cache_tails)


def choose_kernel(held, out_ref, sems_out):
    pieces, rows, _ = held.shape
    wanted = []
    for p in range(pieces):
        wanted.append(jnp.max(held[p, rows - NOTE :, :128].astype(jnp.float32)[7:8]).astype(jnp.int32))
    outof = []
    for p in range(pieces):
        outof.append(pltpu.make_async_copy(held.at[wanted[p]], out_ref.at[p], sems_out.at[p]))
        outof[p].start()
    for copy in outof:
        copy.wait()


def choose(parts):
    pieces = parts.shape[0]
    hbm = pl.BlockSpec(memory_space=pl.ANY)
    return pl.pallas_call(
        choose_kernel,
        out_shape=jax.ShapeDtypeStruct(parts.shape, jnp.bfloat16),
        in_specs=[pl.BlockSpec(memory_space=pltpu.VMEM)],
        out_specs=hbm,
        scratch_shapes=[
            pltpu.SemaphoreType.DMA((pieces,)),
        ],
        compiler_params=pltpu.CompilerParams(vmem_limit_bytes=16 * 1024 * 1024),
        cost_estimate=SMALL,
        name="choose",
    )(parts)


def convolved(extended, weight, bias):
    total = bias + weight[3:4, :] * extended
    for back in range(1, 4):
        total = total + weight[3 - back : 4 - back, :] * pltpu.roll(extended, back, 0)
    return total / (1.0 + jnp.exp(-total))


def local_kernel(
    x_ref, xb_ref, xc_ref, w_ref, wb_ref, wc_ref, b_ref, bb_ref, bc_ref,
    dt_ref, dt_bias_ref, a_log_ref, skip_ref,
    y_ref, fresh_ref, c_out_ref, growth_ref, early_ref, early_carry_ref,
    cum_cols, step_cols, cum_rows, step_rows, carry_cols, scores, b_state,
):
    i = pl.program_id(0)
    rows = SPAN
    t_of = lax.broadcasted_iota(jnp.int32, (rows, rows), 0)
    s_of = lax.broadcasted_iota(jnp.int32, (rows, rows), 1)

    @pl.when(pl.program_id(0) == 0)
    def _():
        v = dt_ref[...] + dt_bias_ref[...]
        step = jnp.maximum(v, 0.0) + jnp.log1p(jnp.exp(-jnp.abs(v)))
        rate = -jnp.exp(a_log_ref[...])
        cum = step * rate
        shift = 1
        while shift < rows:
            cum = cum + jnp.where(t_of >= shift, pltpu.roll(cum, shift, 0), 0.0)
            shift *= 2
        growth_ref[...] = jnp.exp(cum)
        carry = jnp.exp(cum[rows - 1 : rows, :] - cum) * step
        for c in range(CHUNKS):
            cum_cols[c] = cum[:, c * CHUNK_HEADS : (c + 1) * CHUNK_HEADS]
            step_cols[c] = step[:, c * CHUNK_HEADS : (c + 1) * CHUNK_HEADS]
            carry_cols[c] = carry[:, c * CHUNK_HEADS : (c + 1) * CHUNK_HEADS]
        cum_rows[...] = cum.T
        step_rows[...] = step.T

    @pl.when(i % GROUP_CHUNKS == 0)
    def _():
        b_part = convolved(xb_ref[...].astype(jnp.float32), wb_ref, bb_ref[...])
        b_part = jnp.where(t_of >= EARLY, b_part, 0.0).astype(jnp.bfloat16)
        c_part = convolved(xc_ref[...].astype(jnp.float32), wc_ref, bc_ref[...]).astype(jnp.bfloat16)
        b_state[...] = b_part
        c_out_ref[...] = c_part
        both = lax.dot_general(c_part, b_part, (((1,), (1,)), ((), ())), preferred_element_type=jnp.float32)
        scores[...] = jnp.where(t_of >= s_of, both, 0.0)

    x = convolved(x_ref[...].astype(jnp.float32), w_ref, b_ref[...])
    x = jnp.where(lax.broadcasted_iota(jnp.int32, x.shape, 0) >= EARLY, x, 0.0).astype(jnp.bfloat16)
    x32 = x.astype(jnp.float32)
    first = pl.multiple_of(i * CHUNK_HEADS, CHUNK_HEADS)
    cum_r = cum_rows[pl.ds(first, CHUNK_HEADS), :]
    step_r = step_rows[pl.ds(first, CHUNK_HEADS), :]
    cum_c = cum_cols[i]
    carry_c = carry_cols[i]
    low = lax.broadcasted_iota(jnp.int32, (rows, 128), 1) < HEAD_DIM
    zero = jnp.zeros((rows, 128), jnp.bfloat16)
    step_c = step_cols[i]
    t_col = lax.broadcasted_iota(jnp.int32, (rows, CHUNK_HEADS), 0)
    early = []
    for s in range(EARLY):
        decay = jnp.exp(jnp.minimum(cum_c - cum_c[s : s + 1, :], 0.0)) * step_c[s : s + 1, :]
        early.append(jnp.where(t_col >= s, decay, 0.0))
    early = jnp.concatenate(early + [jnp.zeros((rows, CHUNK_HEADS), jnp.float32)], axis=1)
    for c in range(GROUP_CHUNKS):

        @pl.when(i % GROUP_CHUNKS == c)
        def _(c=c):
            early_ref[0, :, c * 4 * CHUNK_HEADS : (c + 1) * 4 * CHUNK_HEADS] = early

    for pair in range(CHUNK_HEADS // 2):
        mixes = []
        for j in (2 * pair, 2 * pair + 1):
            diff = cum_c[:, j : j + 1] - cum_r[j : j + 1, :]
            mixes.append((scores[...] * jnp.exp(jnp.minimum(diff, 0.0)) * step_r[j : j + 1, :]).astype(jnp.bfloat16))
        xp = x[:, pair * 128 : (pair + 1) * 128]
        stacked = jnp.concatenate([jnp.where(low, xp, zero), jnp.where(low, zero, xp)], axis=0)
        y = jnp.dot(jnp.concatenate(mixes, axis=1), stacked, preferred_element_type=jnp.float32)
        cols = slice(pair * 128, (pair + 1) * 128)
        y_ref[:, cols] = y + skip_ref[:, cols] * x32[:, cols]
        weight = jnp.where(low, carry_c[:, 2 * pair : 2 * pair + 1], carry_c[:, 2 * pair + 1 : 2 * pair + 2])
        early_carry_ref[:, cols] = weight[:8]
        carried = (weight * x32[:, cols]).astype(jnp.bfloat16)
        fresh_ref[:, cols] = lax.dot_general(
            b_state[...], carried, (((0,), (0,)), ((), ())), preferred_element_type=jnp.float32
        )


def local_part(xbc, conv_weight, conv_bias, dt_raw, dt_bias, a_log, skip):
    rows = xbc.shape[0]
    bias = conv_bias[None, :]
    first_b = INNER // 128

    def blocks(height):
        return [
            pl.BlockSpec((height, CHUNK), lambda i: (0, i)),
            pl.BlockSpec((height, 128), lambda i: (0, first_b + i // GROUP_CHUNKS)),
            pl.BlockSpec((height, 128), lambda i: (0, first_b + GROUPS + i // GROUP_CHUNKS)),
        ]

    whole = lambda *shape: pl.BlockSpec(shape, lambda i: (0, 0))
    return pl.pallas_call(
        local_kernel,
        grid=(CHUNKS,),
        out_shape=(
            pltpu.HBM((rows, INNER), jnp.float32),
            pltpu.HBM((NST, INNER), jnp.float32),
            pltpu.HBM((rows, GROUPS * NST), jnp.bfloat16),
            pltpu.HBM((rows, HEADS), jnp.float32),
            pltpu.HBM((GROUPS, rows, 128), jnp.float32),
            pltpu.HBM((8, INNER), jnp.float32),
        ),
        in_specs=blocks(rows) + blocks(4) + blocks(1)
        + [whole(rows, HEADS), whole(1, HEADS), whole(1, HEADS), pl.BlockSpec((1, CHUNK), lambda i: (0, i))],
        out_specs=(
            pl.BlockSpec((rows, CHUNK), lambda i: (0, i)),
            pl.BlockSpec((NST, CHUNK), lambda i: (0, i)),
            pl.BlockSpec((rows, NST), lambda i: (0, i // GROUP_CHUNKS)),
            whole(rows, HEADS),
            pl.BlockSpec((1, rows, 128), lambda i: (i // GROUP_CHUNKS, 0, 0)),
            pl.BlockSpec((8, CHUNK), lambda i: (0, i)),
        ),
        scratch_shapes=[
            pltpu.VMEM((CHUNKS, rows, CHUNK_HEADS), jnp.float32),
            pltpu.VMEM((CHUNKS, rows, CHUNK_HEADS), jnp.float32),
            pltpu.VMEM((HEADS, rows), jnp.float32),
            pltpu.VMEM((HEADS, rows), jnp.float32),
            pltpu.VMEM((CHUNKS, rows, CHUNK_HEADS), jnp.float32),
            pltpu.VMEM((rows, rows), jnp.float32),
            pltpu.VMEM((rows, NST), jnp.bfloat16),
        ],
        compiler_params=pltpu.CompilerParams(vmem_limit_bytes=60 * 1024 * 1024),
        cost_estimate=pl.CostEstimate(flops=1000, bytes_accessed=1000, transcendentals=0),
        name="local_part",
    )(
        xbc, xbc, xbc, conv_weight, conv_weight, conv_weight, bias, bias, bias,
        dt_raw, dt_bias[None, :], a_log[None, :], skip,
    )


def state_kernel(
    live_ref, start_ref, xbc_ref, c_hbm, growth_hbm, early_hbm, carry_hbm, channel_hbm, y_ref, fresh_ref,
    y_out_ref, final_ref,
    raw, x_in, c_ref, growth_ref, early_ref, early_carry_ref, channel_ref,
    y_in, fresh_in, y_done, final_done, tail, c_full, sems, sems_raw, sems_in, sems_out,
):
    pieces, height, width = raw.shape
    split = height // NST
    blocks = GROUP // width
    share = (CHANNELS - INNER) // pieces
    live = live_ref[0] > 0
    starts = [pltpu.make_async_copy(start_ref.at[p], raw.at[p], sems_raw.at[p]) for p in range(pieces)]
    small = (
        (xbc_ref.at[pl.ds(0, 16)], x_in), (channel_hbm, channel_ref), (c_hbm, c_ref), (growth_hbm, growth_ref),
        (early_hbm, early_ref), (carry_hbm, early_carry_ref),
    )
    small = [pltpu.make_async_copy(a, b, sems.at[n]) for n, (a, b) in enumerate(small)]
    into, outof = [], []
    for g in range(GROUPS):
        columns = pl.ds(g * GROUP, GROUP)
        into.append(
            (
                pltpu.make_async_copy(y_ref.at[:, columns], y_in.at[g], sems_in.at[g, 0]),
                pltpu.make_async_copy(fresh_ref.at[:, columns], fresh_in.at[g], sems_in.at[g, 1]),
            )
        )
        outof += [
            pltpu.make_async_copy(y_done.at[g], y_out_ref.at[:, columns], sems_out.at[g, 0]),
            pltpu.make_async_copy(final_done.at[g], final_ref.at[0, :, columns], sems_out.at[g, 1]),
        ]
    for copy in small + starts:
        copy.start()
    for copies in into[:2]:
        for copy in copies:
            copy.start()
    tail[...] = jnp.zeros(tail.shape, jnp.float32)
    for copy in starts:
        copy.wait()
    for copies in into[2:]:
        for copy in copies:
            copy.start()
    for p in range(pieces):
        note = raw[p, split * NST :, :].astype(jnp.float32)
        note = jnp.where(live, note, 0.0)
        for k in range(split):
            first = (p * split + k) * width
            tail[5:8, first : first + width] = note[k * EARLY : (k + 1) * EARLY, :]
        first = INNER + p * share
        for r in range(EARLY):
            tail[5 + r : 6 + r, first : first + share] = note[6:7, r * share : (r + 1) * share]
    for copy in small:
        copy.wait()

    def early_rows(first, size):
        here = slice(first, first + size)
        extended = jnp.concatenate([tail[:, here], x_in[:, here].astype(jnp.float32)[:8]], axis=0)
        rows = convolved(extended, channel_ref[:4, here], channel_ref[4:5, here])[8:]
        rows = jnp.where(lax.broadcasted_iota(jnp.int32, rows.shape, 0) < EARLY, rows, 0.0)
        return rows.astype(jnp.bfloat16).astype(jnp.float32)

    def padded(rows):
        return jnp.concatenate([rows, jnp.zeros_like(rows)], axis=0).astype(jnp.bfloat16)

    b_early = early_rows(INNER, GROUPS * NST)
    c_early = padded(early_rows(INNER + GROUPS * NST, GROUPS * NST))
    c_full[...] = c_ref[...]
    sixteen = lax.broadcasted_iota(jnp.int32, c_early.shape, 0)
    c_full[:16, :] = jnp.where(sixteen < EARLY, c_early, c_ref[:16, :])

    grown = jnp.where(live, growth_ref[...], 0.0)
    group_head = lax.broadcasted_iota(jnp.int32, (4 * PER_GROUP, width), 0)
    lane_of = lax.broadcasted_iota(jnp.int32, (4 * PER_GROUP, width), 1) // HEAD_DIM
    spreads = []
    for n in range(blocks):
        mine = (group_head % PER_GROUP == lane_of + n * (width // HEAD_DIM)) & (group_head < 3 * PER_GROUP)
        spreads.append(jnp.where(mine, 1.0, 0.0).astype(jnp.bfloat16))
    row = lax.broadcasted_iota(jnp.int32, (128, 128), 0)
    token = row % (4 * CHUNK_HEADS) // CHUNK_HEADS
    own_head = lax.broadcasted_iota(jnp.int32, (CHUNK_HEADS, width), 0)
    lane_head = lax.broadcasted_iota(jnp.int32, (CHUNK_HEADS, width), 1) // HEAD_DIM

    def by_token(of, rows):
        return jnp.where(of == 0, rows[0:1], jnp.where(of == 1, rows[1:2], jnp.where(of == 2, rows[2:3], 0.0)))

    for g in range(GROUPS):
        c_group = c_full[:, g * NST : (g + 1) * NST]
        b_group = b_early[:, g * NST : (g + 1) * NST]
        both = lax.dot_general(
            c_group, by_token(token, b_group).astype(jnp.bfloat16), (((1,), (1,)), ((), ())),
            preferred_element_type=jnp.float32,
        )
        mixing = (both * early_ref[g]).astype(jnp.bfloat16)
        b_group = padded(b_group)
        rest = grown[:, g * PER_GROUP : (g + 1) * PER_GROUP]
        exact = []
        for _ in range(3):
            exact.append(rest.astype(jnp.bfloat16).astype(jnp.float32))
            rest = rest - exact[-1]
        exact = jnp.concatenate(exact + [jnp.zeros_like(rest)], axis=1).astype(jnp.bfloat16)
        for copy in into[g]:
            copy.wait()
        for n in range(blocks):
            first = g * GROUP + n * width
            here, inside = slice(first, first + width), slice(n * width, (n + 1) * width)
            x_early = early_rows(first, width)
            base = first // width % split * NST
            start = raw[first // (split * width), base : base + NST, :]
            y_state = jnp.dot(c_group, start, preferred_element_type=jnp.float32)
            growth = jnp.dot(exact, spreads[n], preferred_element_type=jnp.float32)
            chunk = n * width // CHUNK
            mine = own_head == lane_head + n * width % CHUNK // HEAD_DIM
            inputs = [jnp.where(mine, x_early[s : s + 1], 0.0) for s in range(EARLY)]
            inputs = jnp.concatenate(inputs + [jnp.zeros_like(inputs[0])], axis=0).astype(jnp.bfloat16)
            factors = mixing[:, chunk * 4 * CHUNK_HEADS : (chunk + 1) * 4 * CHUNK_HEADS]
            y = y_in[g, :, inside] + growth * y_state + jnp.dot(factors, inputs, preferred_element_type=jnp.float32)
            skipped = y[:8] + channel_ref[5:6, here] * x_early
            y_done[g, :, inside] = jnp.concatenate([skipped, y[8:]], axis=0).astype(jnp.bfloat16)
            carried = padded(early_carry_ref[:, here] * x_early)
            fresh = fresh_in[g, :, inside] + lax.dot_general(
                b_group, carried, (((0,), (0,)), ((), ())), preferred_element_type=jnp.float32
            )
            kept = growth[SPAN - 1 :, :] * start.astype(jnp.float32)
            final_done[g, :, inside] = (kept + fresh).astype(jnp.bfloat16)
        outof[2 * g].start()
        outof[2 * g + 1].start()
    for copy in outof:
        copy.wait()


def state_part(live, start, xbc, local_results, channels):
    y_local, fresh, c_part, growth, early, early_carry = local_results
    rows = y_local.shape[0]
    hbm = pl.BlockSpec(memory_space=pl.ANY)
    return pl.pallas_call(
        state_kernel,
        out_shape=(
            jax.ShapeDtypeStruct((rows, INNER), jnp.bfloat16),
            jax.ShapeDtypeStruct((1, NST, INNER), jnp.bfloat16),
        ),
        in_specs=[pl.BlockSpec(memory_space=pltpu.SMEM)] + [hbm] * 9,
        out_specs=(hbm, hbm),
        scratch_shapes=[
            pltpu.VMEM(start.shape, jnp.bfloat16),
            pltpu.VMEM((16, CHANNELS), jnp.bfloat16),
            pltpu.VMEM(c_part.shape, c_part.dtype),
            pltpu.VMEM(growth.shape, growth.dtype),
            pltpu.VMEM(early.shape, early.dtype),
            pltpu.VMEM(early_carry.shape, early_carry.dtype),
            pltpu.VMEM(channels.shape, channels.dtype),
            pltpu.VMEM((GROUPS, rows, GROUP), jnp.float32),
            pltpu.VMEM((GROUPS, NST, GROUP), jnp.float32),
            pltpu.VMEM((GROUPS, rows, GROUP), jnp.bfloat16),
            pltpu.VMEM((GROUPS, NST, GROUP), jnp.bfloat16),
            pltpu.VMEM((8, CHANNELS), jnp.float32),
            pltpu.VMEM((rows, GROUPS * NST), jnp.bfloat16),
            pltpu.SemaphoreType.DMA((6,)),
            pltpu.SemaphoreType.DMA((start.shape[0],)),
            pltpu.SemaphoreType.DMA((GROUPS, 2)),
            pltpu.SemaphoreType.DMA((GROUPS, 2)),
        ],
        compiler_params=pltpu.CompilerParams(vmem_limit_bytes=62 * 1024 * 1024),
        cost_estimate=pl.CostEstimate(flops=3 * 134_000_000, bytes_accessed=15_000_000, transcendentals=0),
        name="state_part",
    )(live, start, xbc, c_part, growth, early, early_carry, channels, y_local, fresh)


def local(
    xbc, dt_raw, conv_weight, conv_bias, dt_bias, a_log, d_skip, cache_states, cache_tails,
    hit_owner, hit_slot, hit_spans, request_of,
):
    pieces = hit_owner.shape[0]
    place = lax.axis_index("req").astype(jnp.int32)[None]
    packed = pack(place, hit_owner, hit_slot, request_of, cache_states, cache_tails, pieces)
    parts = lax.all_to_all(packed, "req", split_axis=0, concat_axis=0, tiled=True)
    start = lax.all_to_all(choose(parts), "req", split_axis=0, concat_axis=0, tiled=True)

    live = (hit_spans[request_of[0]] > 0).astype(jnp.int32)[None]
    skip = jnp.repeat(d_skip, HEAD_DIM)[None, :]
    without = local_part(xbc, conv_weight, conv_bias, dt_raw, dt_bias, a_log, skip)
    channels = jnp.concatenate([conv_weight, conv_bias[None, :], jnp.pad(skip, ((0, 3), (0, CHANNELS - INNER)))], axis=0)
    return state_part(live, start, xbc, without, channels)


def solution(mesh):
    in_specs = (
        P(("grp", "req"), None),
        P(("grp", "req"), None),
        P(),
        P(),
        P(),
        P(),
        P(),
        P(("grp", "req"), None, None),
        P(("grp", "req"), None, None),
        P("grp"),
        P("grp"),
        P("grp"),
        P(("grp", "req")),
    )
    out_specs = (P(("grp", "req"), None), P(("grp", "req"), None, None))
    return jax.shard_map(local, mesh=mesh, in_specs=in_specs, out_specs=out_specs, check_vma=False)
```

```python
import functools

import jax
import jax.numpy as jnp
from jax import lax
from jax.experimental import pallas as pl
from jax.experimental.pallas import tpu as pltpu
from jax.sharding import PartitionSpec as P

HEADS = 128
HEAD_DIM = 64
GROUPS = 4
NST = 128
INNER = 8192
SPAN = 128
PER_GROUP = HEADS // GROUPS
CHUNK = 512
CHUNK_HEADS = CHUNK // HEAD_DIM
CHUNKS = INNER // CHUNK
GROUP_CHUNKS = CHUNKS // GROUPS
CHANNELS = INNER + 2 * GROUPS * NST
EARLY = 3
GROUP = INNER // GROUPS
NOTE = 8
SMALL = pl.CostEstimate(flops=1000, bytes_accessed=1000, transcendentals=0)


def served_slot(device, owner_ref, slot_ref):
    served = jnp.int32(0)
    for r in range(owner_ref.shape[0]):
        served = jnp.where(owner_ref[r] == device, jnp.maximum(served, slot_ref[r]), served)
    return served


def piece_shape(pieces):
    width = INNER // pieces
    split = 2 if width >= 256 else 1
    return split, width // split


def pack_kernel(
    device_ref, owner_ref, slot_ref, request_ref, cache_ref, tails_ref, held, tail, note, sems_in, sem
):
    pieces = held.shape[0]
    split, width = piece_shape(pieces)
    share = (CHANNELS - INNER) // pieces
    served = served_slot(device_ref[0], owner_ref, slot_ref)
    tail_copy = pltpu.make_async_copy(tails_ref.at[served], tail, sem)
    into = []
    for p in range(pieces):
        for k in range(split):
            source = cache_ref.at[served, :, pl.ds((p * split + k) * width, width)]
            into.append(pltpu.make_async_copy(source, held.at[p, pl.ds(k * NST, NST)], sems_in.at[p, k]))
    tail_copy.start()
    for copy in into:
        copy.start()
    note[...] = jnp.zeros(note.shape, jnp.float32)
    note[7:8, :] = jnp.full((1, width), owner_ref[request_ref[0]].astype(jnp.float32))
    tail_copy.wait()
    last = tail[...].astype(jnp.float32)
    taps = last.shape[0]
    for p in range(pieces):
        for k in range(split):
            first = (p * split + k) * width
            note[k * taps : (k + 1) * taps, :] = last[:, first : first + width]
        first = INNER + p * share
        shares = [last[r : r + 1, first : first + share] for r in range(taps)]
        shares.append(jnp.zeros((1, width - taps * share), jnp.float32))
        note[6:7, :] = jnp.concatenate(shares, axis=1)
        held[p, split * NST :, :] = note[...].astype(jnp.bfloat16)
    for copy in into:
        copy.wait()


def pack(device, hit_owner, hit_slot, request_of, cache_states, cache_tails, pieces):
    smem = pl.BlockSpec(memory_space=pltpu.SMEM)
    hbm = pl.BlockSpec(memory_space=pl.ANY)
    split, width = piece_shape(pieces)
    shape = (pieces, split * NST + NOTE, width)
    return pl.pallas_call(
        pack_kernel,
        out_shape=pltpu.VMEM(shape, jnp.bfloat16),
        in_specs=[smem] * 4 + [hbm, hbm],
        out_specs=pl.BlockSpec(memory_space=pltpu.VMEM),
        scratch_shapes=[
            pltpu.VMEM(cache_tails.shape[1:], jnp.bfloat16),
            pltpu.VMEM((NOTE, width), jnp.float32),
            pltpu.SemaphoreType.DMA((pieces, split)),
            pltpu.SemaphoreType.DMA,
        ],
        compiler_params=pltpu.CompilerParams(vmem_limit_bytes=56 * 1024 * 1024),
        cost_estimate=SMALL,
        name="pack",
    )(device, hit_owner, hit_slot, request_of, cache_states, cache_tails)


def choose_kernel(held, out_ref, sems_out):
    pieces, rows, _ = held.shape
    wanted = []
    for p in range(pieces):
        wanted.append(jnp.max(held[p, rows - NOTE :, :128].astype(jnp.float32)[7:8]).astype(jnp.int32))
    outof = []
    for p in range(pieces):
        outof.append(pltpu.make_async_copy(held.at[wanted[p]], out_ref.at[p], sems_out.at[p]))
        outof[p].start()
    for copy in outof:
        copy.wait()


def choose(parts):
    pieces = parts.shape[0]
    hbm = pl.BlockSpec(memory_space=pl.ANY)
    return pl.pallas_call(
        choose_kernel,
        out_shape=jax.ShapeDtypeStruct(parts.shape, jnp.bfloat16),
        in_specs=[pl.BlockSpec(memory_space=pltpu.VMEM)],
        out_specs=hbm,
        scratch_shapes=[
            pltpu.SemaphoreType.DMA((pieces,)),
        ],
        compiler_params=pltpu.CompilerParams(vmem_limit_bytes=16 * 1024 * 1024),
        cost_estimate=SMALL,
        name="choose",
    )(parts)


def convolved(extended, weight, bias):
    total = bias + weight[3:4, :] * extended
    for back in range(1, 4):
        total = total + weight[3 - back : 4 - back, :] * pltpu.roll(extended, back, 0)
    return total / (1.0 + jnp.exp(-total))


def local_kernel(
    x_ref, xb_ref, xc_ref, w_ref, wb_ref, wc_ref, b_ref, bb_ref, bc_ref,
    dt_ref, dt_bias_ref, a_log_ref, skip_ref,
    y_ref, fresh_ref, c_out_ref, growth_ref, early_ref, early_carry_ref,
    cum_cols, step_cols, cum_rows, step_rows, carry_cols, scores, b_state,
):
    i = pl.program_id(0)
    rows = SPAN
    t_of = lax.broadcasted_iota(jnp.int32, (rows, rows), 0)
    s_of = lax.broadcasted_iota(jnp.int32, (rows, rows), 1)

    @pl.when(pl.program_id(0) == 0)
    def _():
        v = dt_ref[...] + dt_bias_ref[...]
        step = jnp.maximum(v, 0.0) + jnp.log1p(jnp.exp(-jnp.abs(v)))
        rate = -jnp.exp(a_log_ref[...])
        cum = step * rate
        shift = 1
        while shift < rows:
            cum = cum + jnp.where(t_of >= shift, pltpu.roll(cum, shift, 0), 0.0)
            shift *= 2
        growth_ref[...] = jnp.exp(cum)
        carry = jnp.exp(cum[rows - 1 : rows, :] - cum) * step
        for c in range(CHUNKS):
            cum_cols[c] = cum[:, c * CHUNK_HEADS : (c + 1) * CHUNK_HEADS]
            step_cols[c] = step[:, c * CHUNK_HEADS : (c + 1) * CHUNK_HEADS]
            carry_cols[c] = carry[:, c * CHUNK_HEADS : (c + 1) * CHUNK_HEADS]
        cum_rows[...] = cum.T
        step_rows[...] = step.T

    @pl.when(i % GROUP_CHUNKS == 0)
    def _():
        b_part = convolved(xb_ref[...].astype(jnp.float32), wb_ref, bb_ref[...])
        b_part = jnp.where(t_of >= EARLY, b_part, 0.0).astype(jnp.bfloat16)
        c_part = convolved(xc_ref[...].astype(jnp.float32), wc_ref, bc_ref[...]).astype(jnp.bfloat16)
        b_state[...] = b_part
        c_out_ref[...] = c_part
        both = lax.dot_general(c_part, b_part, (((1,), (1,)), ((), ())), preferred_element_type=jnp.float32)
        scores[...] = jnp.where(t_of >= s_of, both, 0.0)

    x = convolved(x_ref[...].astype(jnp.float32), w_ref, b_ref[...])
    x = jnp.where(lax.broadcasted_iota(jnp.int32, x.shape, 0) >= EARLY, x, 0.0).astype(jnp.bfloat16)
    x32 = x.astype(jnp.float32)
    first = pl.multiple_of(i * CHUNK_HEADS, CHUNK_HEADS)
    cum_r = cum_rows[pl.ds(first, CHUNK_HEADS), :]
    step_r = step_rows[pl.ds(first, CHUNK_HEADS), :]
    cum_c = cum_cols[i]
    carry_c = carry_cols[i]
    low = lax.broadcasted_iota(jnp.int32, (rows, 128), 1) < HEAD_DIM
    zero = jnp.zeros((rows, 128), jnp.bfloat16)
    step_c = step_cols[i]
    t_col = lax.broadcasted_iota(jnp.int32, (rows, CHUNK_HEADS), 0)
    early = []
    for s in range(EARLY):
        decay = jnp.exp(jnp.minimum(cum_c - cum_c[s : s + 1, :], 0.0)) * step_c[s : s + 1, :]
        early.append(jnp.where(t_col >= s, decay, 0.0))
    early = jnp.concatenate(early + [jnp.zeros((rows, CHUNK_HEADS), jnp.float32)], axis=1)
    for c in range(GROUP_CHUNKS):

        @pl.when(i % GROUP_CHUNKS == c)
        def _(c=c):
            early_ref[0, :, c * 4 * CHUNK_HEADS : (c + 1) * 4 * CHUNK_HEADS] = early

    for pair in range(CHUNK_HEADS // 2):
        mixes = []
        for j in (2 * pair, 2 * pair + 1):
            diff = cum_c[:, j : j + 1] - cum_r[j : j + 1, :]
            mixes.append((scores[...] * jnp.exp(jnp.minimum(diff, 0.0)) * step_r[j : j + 1, :]).astype(jnp.bfloat16))
        xp = x[:, pair * 128 : (pair + 1) * 128]
        stacked = jnp.concatenate([jnp.where(low, xp, zero), jnp.where(low, zero, xp)], axis=0)
        y = jnp.dot(jnp.concatenate(mixes, axis=1), stacked, preferred_element_type=jnp.float32)
        cols = slice(pair * 128, (pair + 1) * 128)
        y_ref[:, cols] = y + skip_ref[:, cols] * x32[:, cols]
        weight = jnp.where(low, carry_c[:, 2 * pair : 2 * pair + 1], carry_c[:, 2 * pair + 1 : 2 * pair + 2])
        early_carry_ref[:, cols] = weight[:8]
        carried = (weight * x32[:, cols]).astype(jnp.bfloat16)
        fresh_ref[:, cols] = lax.dot_general(
            b_state[...], carried, (((0,), (0,)), ((), ())), preferred_element_type=jnp.float32
        )


def local_part(xbc, conv_weight, conv_bias, dt_raw, dt_bias, a_log, skip):
    rows = xbc.shape[0]
    bias = conv_bias[None, :]
    first_b = INNER // 128

    def blocks(height):
        return [
            pl.BlockSpec((height, CHUNK), lambda i: (0, i)),
            pl.BlockSpec((height, 128), lambda i: (0, first_b + i // GROUP_CHUNKS)),
            pl.BlockSpec((height, 128), lambda i: (0, first_b + GROUPS + i // GROUP_CHUNKS)),
        ]

    whole = lambda *shape: pl.BlockSpec(shape, lambda i: (0, 0))
    return pl.pallas_call(
        local_kernel,
        grid=(CHUNKS,),
        out_shape=(
            pltpu.HBM((rows, INNER), jnp.float32),
            pltpu.HBM((NST, INNER), jnp.float32),
            pltpu.HBM((rows, GROUPS * NST), jnp.bfloat16),
            pltpu.HBM((rows, HEADS), jnp.float32),
            pltpu.HBM((GROUPS, rows, 128), jnp.float32),
            pltpu.HBM((8, INNER), jnp.float32),
        ),
        in_specs=blocks(rows) + blocks(4) + blocks(1)
        + [whole(rows, HEADS), whole(1, HEADS), whole(1, HEADS), pl.BlockSpec((1, CHUNK), lambda i: (0, i))],
        out_specs=(
            pl.BlockSpec((rows, CHUNK), lambda i: (0, i)),
            pl.BlockSpec((NST, CHUNK), lambda i: (0, i)),
            pl.BlockSpec((rows, NST), lambda i: (0, i // GROUP_CHUNKS)),
            whole(rows, HEADS),
            pl.BlockSpec((1, rows, 128), lambda i: (i // GROUP_CHUNKS, 0, 0)),
            pl.BlockSpec((8, CHUNK), lambda i: (0, i)),
        ),
        scratch_shapes=[
            pltpu.VMEM((CHUNKS, rows, CHUNK_HEADS), jnp.float32),
            pltpu.VMEM((CHUNKS, rows, CHUNK_HEADS), jnp.float32),
            pltpu.VMEM((HEADS, rows), jnp.float32),
            pltpu.VMEM((HEADS, rows), jnp.float32),
            pltpu.VMEM((CHUNKS, rows, CHUNK_HEADS), jnp.float32),
            pltpu.VMEM((rows, rows), jnp.float32),
            pltpu.VMEM((rows, NST), jnp.bfloat16),
        ],
        compiler_params=pltpu.CompilerParams(vmem_limit_bytes=60 * 1024 * 1024),
        cost_estimate=pl.CostEstimate(flops=1000, bytes_accessed=1000, transcendentals=0),
        name="local_part",
    )(
        xbc, xbc, xbc, conv_weight, conv_weight, conv_weight, bias, bias, bias,
        dt_raw, dt_bias[None, :], a_log[None, :], skip,
    )


def state_kernel(
    live_ref, start_ref, xbc_ref, c_hbm, growth_hbm, early_hbm, carry_hbm, channel_hbm, y_ref, fresh_ref,
    y_out_ref, final_ref,
    raw, x_in, c_ref, growth_ref, early_ref, early_carry_ref, channel_ref,
    y_in, fresh_in, y_done, final_done, tail, c_full, sems, sems_raw, sems_in, sems_out,
):
    pieces, height, width = raw.shape
    split = height // NST
    blocks = GROUP // width
    share = (CHANNELS - INNER) // pieces
    live = live_ref[0] > 0
    starts = [pltpu.make_async_copy(start_ref.at[p], raw.at[p], sems_raw.at[p]) for p in range(pieces)]
    small = (
        (xbc_ref.at[pl.ds(0, 16)], x_in), (channel_hbm, channel_ref), (c_hbm, c_ref), (growth_hbm, growth_ref),
        (early_hbm, early_ref), (carry_hbm, early_carry_ref),
    )
    small = [pltpu.make_async_copy(a, b, sems.at[n]) for n, (a, b) in enumerate(small)]
    into, outof = [], []
    for g in range(GROUPS):
        columns = pl.ds(g * GROUP, GROUP)
        into.append(
            (
                pltpu.make_async_copy(y_ref.at[:, columns], y_in.at[g], sems_in.at[g, 0]),
                pltpu.make_async_copy(fresh_ref.at[:, columns], fresh_in.at[g], sems_in.at[g, 1]),
            )
        )
        outof += [
            pltpu.make_async_copy(y_done.at[g], y_out_ref.at[:, columns], sems_out.at[g, 0]),
            pltpu.make_async_copy(final_done.at[g], final_ref.at[0, :, columns], sems_out.at[g, 1]),
        ]
    for copy in small + starts:
        copy.start()
    for copies in into[:2]:
        for copy in copies:
            copy.start()
    tail[...] = jnp.zeros(tail.shape, jnp.float32)
    for copy in starts:
        copy.wait()
    for copies in into[2:]:
        for copy in copies:
            copy.start()
    for p in range(pieces):
        note = raw[p, split * NST :, :].astype(jnp.float32)
        note = jnp.where(live, note, 0.0)
        for k in range(split):
            first = (p * split + k) * width
            tail[5:8, first : first + width] = note[k * EARLY : (k + 1) * EARLY, :]
        first = INNER + p * share
        for r in range(EARLY):
            tail[5 + r : 6 + r, first : first + share] = note[6:7, r * share : (r + 1) * share]
    for copy in small:
        copy.wait()

    def early_rows(first, size):
        here = slice(first, first + size)
        extended = jnp.concatenate([tail[:, here], x_in[:, here].astype(jnp.float32)[:8]], axis=0)
        rows = convolved(extended, channel_ref[:4, here], channel_ref[4:5, here])[8:]
        rows = jnp.where(lax.broadcasted_iota(jnp.int32, rows.shape, 0) < EARLY, rows, 0.0)
        return rows.astype(jnp.bfloat16).astype(jnp.float32)

    def padded(rows):
        return jnp.concatenate([rows, jnp.zeros_like(rows)], axis=0).astype(jnp.bfloat16)

    b_early = early_rows(INNER, GROUPS * NST)
    c_early = padded(early_rows(INNER + GROUPS * NST, GROUPS * NST))
    c_full[...] = c_ref[...]
    sixteen = lax.broadcasted_iota(jnp.int32, c_early.shape, 0)
    c_full[:16, :] = jnp.where(sixteen < EARLY, c_early, c_ref[:16, :])

    grown = jnp.where(live, growth_ref[...], 0.0)
    group_head = lax.broadcasted_iota(jnp.int32, (4 * PER_GROUP, width), 0)
    lane_of = lax.broadcasted_iota(jnp.int32, (4 * PER_GROUP, width), 1) // HEAD_DIM
    spreads = []
    for n in range(blocks):
        mine = (group_head % PER_GROUP == lane_of + n * (width // HEAD_DIM)) & (group_head < 3 * PER_GROUP)
        spreads.append(jnp.where(mine, 1.0, 0.0).astype(jnp.bfloat16))
    row = lax.broadcasted_iota(jnp.int32, (128, 128), 0)
    token = row % (4 * CHUNK_HEADS) // CHUNK_HEADS
    own_head = lax.broadcasted_iota(jnp.int32, (CHUNK_HEADS, width), 0)
    lane_head = lax.broadcasted_iota(jnp.int32, (CHUNK_HEADS, width), 1) // HEAD_DIM

    def by_token(of, rows):
        return jnp.where(of == 0, rows[0:1], jnp.where(of == 1, rows[1:2], jnp.where(of == 2, rows[2:3], 0.0)))

    for g in range(GROUPS):
        c_group = c_full[:, g * NST : (g + 1) * NST]
        b_group = b_early[:, g * NST : (g + 1) * NST]
        both = lax.dot_general(
            c_group, by_token(token, b_group).astype(jnp.bfloat16), (((1,), (1,)), ((), ())),
            preferred_element_type=jnp.float32,
        )
        mixing = (both * early_ref[g]).astype(jnp.bfloat16)
        b_group = padded(b_group)
        rest = grown[:, g * PER_GROUP : (g + 1) * PER_GROUP]
        exact = []
        for _ in range(3):
            exact.append(rest.astype(jnp.bfloat16).astype(jnp.float32))
            rest = rest - exact[-1]
        exact = jnp.concatenate(exact + [jnp.zeros_like(rest)], axis=1).astype(jnp.bfloat16)
        for copy in into[g]:
            copy.wait()
        for n in range(blocks):
            first = g * GROUP + n * width
            here, inside = slice(first, first + width), slice(n * width, (n + 1) * width)
            x_early = early_rows(first, width)
            base = first // width % split * NST
            start = raw[first // (split * width), base : base + NST, :]
            y_state = jnp.dot(c_group, start, preferred_element_type=jnp.float32)
            growth = jnp.dot(exact, spreads[n], preferred_element_type=jnp.float32)
            chunk = n * width // CHUNK
            mine = own_head == lane_head + n * width % CHUNK // HEAD_DIM
            inputs = [jnp.where(mine, x_early[s : s + 1], 0.0) for s in range(EARLY)]
            inputs = jnp.concatenate(inputs + [jnp.zeros_like(inputs[0])], axis=0).astype(jnp.bfloat16)
            factors = mixing[:, chunk * 4 * CHUNK_HEADS : (chunk + 1) * 4 * CHUNK_HEADS]
            y = y_in[g, :, inside] + growth * y_state + jnp.dot(factors, inputs, preferred_element_type=jnp.float32)
            skipped = y[:8] + channel_ref[5:6, here] * x_early
            y_done[g, :, inside] = jnp.concatenate([skipped, y[8:]], axis=0).astype(jnp.bfloat16)
            carried = padded(early_carry_ref[:, here] * x_early)
            fresh = fresh_in[g, :, inside] + lax.dot_general(
                b_group, carried, (((0,), (0,)), ((), ())), preferred_element_type=jnp.float32
            )
            kept = growth[SPAN - 1 :, :] * start.astype(jnp.float32)
            final_done[g, :, inside] = (kept + fresh).astype(jnp.bfloat16)
        outof[2 * g].start()
        outof[2 * g + 1].start()
    for copy in outof:
        copy.wait()


def state_part(live, start, xbc, local_results, channels):
    y_local, fresh, c_part, growth, early, early_carry = local_results
    rows = y_local.shape[0]
    hbm = pl.BlockSpec(memory_space=pl.ANY)
    return pl.pallas_call(
        state_kernel,
        out_shape=(
            jax.ShapeDtypeStruct((rows, INNER), jnp.bfloat16),
            jax.ShapeDtypeStruct((1, NST, INNER), jnp.bfloat16),
        ),
        in_specs=[pl.BlockSpec(memory_space=pltpu.SMEM)] + [hbm] * 9,
        out_specs=(hbm, hbm),
        scratch_shapes=[
            pltpu.VMEM(start.shape, jnp.bfloat16),
            pltpu.VMEM((16, CHANNELS), jnp.bfloat16),
            pltpu.VMEM(c_part.shape, c_part.dtype),
            pltpu.VMEM(growth.shape, growth.dtype),
            pltpu.VMEM(early.shape, early.dtype),
            pltpu.VMEM(early_carry.shape, early_carry.dtype),
            pltpu.VMEM(channels.shape, channels.dtype),
            pltpu.VMEM((GROUPS, rows, GROUP), jnp.float32),
            pltpu.VMEM((GROUPS, NST, GROUP), jnp.float32),
            pltpu.VMEM((GROUPS, rows, GROUP), jnp.bfloat16),
            pltpu.VMEM((GROUPS, NST, GROUP), jnp.bfloat16),
            pltpu.VMEM((8, CHANNELS), jnp.float32),
            pltpu.VMEM((rows, GROUPS * NST), jnp.bfloat16),
            pltpu.SemaphoreType.DMA((6,)),
            pltpu.SemaphoreType.DMA((start.shape[0],)),
            pltpu.SemaphoreType.DMA((GROUPS, 2)),
            pltpu.SemaphoreType.DMA((GROUPS, 2)),
        ],
        compiler_params=pltpu.CompilerParams(vmem_limit_bytes=62 * 1024 * 1024),
        cost_estimate=pl.CostEstimate(flops=3 * 134_000_000, bytes_accessed=15_000_000, transcendentals=0),
        name="state_part",
    )(live, start, xbc, c_part, growth, early, early_carry, channels, y_local, fresh)


def local(
    xbc, dt_raw, conv_weight, conv_bias, dt_bias, a_log, d_skip, cache_states, cache_tails,
    hit_owner, hit_slot, hit_spans, request_of,
):
    pieces = hit_owner.shape[0]
    place = lax.axis_index("req").astype(jnp.int32)[None]
    packed = pack(place, hit_owner, hit_slot, request_of, cache_states, cache_tails, pieces)
    parts = lax.all_to_all(packed, "req", split_axis=0, concat_axis=0, tiled=True)
    start = lax.all_to_all(choose(parts), "req", split_axis=0, concat_axis=0, tiled=True)

    live = (hit_spans[request_of[0]] > 0).astype(jnp.int32)[None]
    skip = jnp.repeat(d_skip, HEAD_DIM)[None, :]
    without = local_part(xbc, conv_weight, conv_bias, dt_raw, dt_bias, a_log, skip)
    channels = jnp.concatenate([conv_weight, conv_bias[None, :], jnp.pad(skip, ((0, 3), (0, CHANNELS - INNER)))], axis=0)
    return state_part(live, start, xbc, without, channels)


def solution(mesh):
    in_specs = (
        P(("grp", "req"), None),
        P(("grp", "req"), None),
        P(),
        P(),
        P(),
        P(),
        P(),
        P(("grp", "req"), None, None),
        P(("grp", "req"), None, None),
        P("grp"),
        P("grp"),
        P("grp"),
        P(("grp", "req")),
    )
    out_specs = (P(("grp", "req"), None), P(("grp", "req"), None, None))
    return jax.shard_map(local, mesh=mesh, in_specs=in_specs, out_specs=out_specs, check_vma=False)
```
